32 devices in a mesh: seq: 16 (over z, y, core), col: 2 (over x).
Axes of the slice: x: 2, y: 2, z: 4, core: 2. Of those that a mesh axis runs over, the one named last changes fastest.
Arguments:
- memory: bfloat16 [2048, 4096], P('col', 'seq'), may hold values from -8 to 8
- query: bfloat16 [4096, 2048], P('seq', 'col'), may hold values from -400 to 400
- out_grad: bfloat16 [4096, 2048], P('seq', 'col'), may hold values from -96 to 96
- w_key: bfloat16 [4096, 2048], P(None, 'col'), may hold values from -0.09375 to 0.09375
- w_value: bfloat16 [4096, 2048], P(None, 'col'), may hold values from -0.09375 to 0.09375
Outputs:
- d_query: bfloat16 [4096, 2048], P('seq', 'col')
- d_memory: bfloat16 [2048, 4096], P('col', 'seq')
The draws below stay inside these ranges and needn't reach their ends.
All inputs are finite; a program needn't handle non-finite values.
Results may differ from the reference program's by a relative error of at most 0.02.
The reference program's roundings to bfloat16 on the way (of `key_rows`, `value_rows`, `weights_low`, `score_grad`, `key_grad` and `value_grad`) count: a program that leaves them out, or rounds other values in their place, can miss the bound.
Values may be sent and summed in bfloat16 or wider, within the bound.
No kernel may reach another device: no remote copies, remote signals or barrier semaphores. Data moves between devices by JAX's collectives and lax.ppermute only.
A program may use at most 128 MiB of HBM per device.

```python
import math
import jax
import jax.numpy as jnp
from jax import lax

D = 4096
HD = 64
HEADS = 32
INNER = 2048
SRC = 2048
TGT = 4096


def shared_draws(key):
    memory = jax.random.truncated_normal(jax.random.fold_in(key, 101), -6.0, 6.0, (SRC, D), jnp.float32)
    w_key = jax.random.truncated_normal(jax.random.fold_in(key, 102), -6.0, 6.0, (D, INNER), jnp.float32) * D ** (-0.5)
    query = jax.random.truncated_normal(jax.random.fold_in(key, 103), -6.0, 6.0, (TGT, INNER), jnp.float32)
    return (memory, w_key, query)


def draw_memory(key, part):
    return shared_draws(key)[0].astype(jnp.bfloat16)


def draw_w_key(key, part):
    return shared_draws(key)[1].astype(jnp.bfloat16)


def draw_query(key, part):
    return shared_draws(key)[2].astype(jnp.bfloat16)


def steps_of(own_key, extent, split, least, high):
    loudness, own = 1.0, jax.random.fold_in(own_key, 6)
    for axis_at, blocks in split:
        draws = jnp.exp(jax.random.uniform(jax.random.fold_in(own, axis_at), (blocks,), jnp.float32, least / len(split), high / len(split)))
        loudness = loudness * jnp.repeat(draws, extent[axis_at] // blocks).reshape([-1 if axis == axis_at else 1 for axis in range(len(extent))])
    return loudness


def centred(rng, dims, deviation, reach, pieces=(), held_as=jnp.bfloat16):
    loudness = steps_of(rng, dims, pieces, -0.22, 0.18) if pieces else 1.0
    entries = jax.random.normal(rng, dims, jnp.float32) * deviation * loudness
    return jnp.minimum(jnp.maximum(entries, -reach), reach).astype(held_as)


def setup_inputs(seed: int = 0) -> dict:
    seeds = jax.random.split(jax.random.key(seed), 6)
    memory = draw_memory(jax.random.fold_in(seeds[5], 71), 0)
    query = draw_query(jax.random.fold_in(seeds[5], 71), 0)
    out_grad = centred(seeds[2], (TGT, INNER), 16.0, 96.0, ((0, 16), (1, 2)))
    w_key = draw_w_key(jax.random.fold_in(seeds[5], 71), 0)
    w_value = centred(seeds[4], (D, INNER), D ** -0.5, 0.09375, ((1, 2),))
    return dict(memory=memory, query=query, out_grad=out_grad, w_key=w_key, w_value=w_value)


def head_grads(query_head, grad_head, key_head, value_head):
    factor = 1.0 / math.sqrt(HD)
    block_rows = math.gcd(TGT, 2048)
    query_blocks = query_head.reshape(TGT // block_rows, block_rows, HD)
    grad_blocks = grad_head.reshape(TGT // block_rows, block_rows, HD)

    def advance(totals, pair):
        query_block, grad_block = pair
        scores = jnp.dot(query_block, key_head.T, preferred_element_type=jnp.float32) * factor
        weights = jax.nn.softmax(scores, axis=-1)
        weights_low = weights.astype(jnp.bfloat16)
        attended = jnp.dot(weights_low, value_head, preferred_element_type=jnp.float32)
        row_delta = lax.optimization_barrier(jnp.sum(grad_block.astype(jnp.float32) * attended, axis=-1, keepdims=True))
        prob_grad = jnp.dot(grad_block, value_head.T, preferred_element_type=jnp.float32)
        score_grad = (weights * (prob_grad - row_delta) * factor).astype(jnp.bfloat16)
        query_grad = jnp.dot(score_grad, key_head, preferred_element_type=jnp.float32).astype(jnp.bfloat16)
        key_total = totals[0] + jnp.dot(score_grad.T, query_block, preferred_element_type=jnp.float32)
        value_total = totals[1] + jnp.dot(weights_low.T, grad_block, preferred_element_type=jnp.float32)
        return ((key_total, value_total), query_grad)
    start = (jnp.zeros((SRC, HD), jnp.float32), jnp.zeros((SRC, HD), jnp.float32))
    totals, query_grad = lax.scan(advance, start, (query_blocks, grad_blocks))
    return (query_grad.reshape(TGT, HD), totals[0], totals[1])

def reference(memory, query, out_grad, w_key, w_value):
    key_rows = jnp.dot(memory, w_key, preferred_element_type=jnp.float32).astype(jnp.bfloat16)
    value_rows = jnp.dot(memory, w_value, preferred_element_type=jnp.float32).astype(jnp.bfloat16)
    query_heads = query.reshape(TGT, HEADS, HD).transpose(1, 0, 2)
    grad_heads = out_grad.reshape(TGT, HEADS, HD).transpose(1, 0, 2)
    key_heads = key_rows.reshape(SRC, HEADS, HD).transpose(1, 0, 2)
    value_heads = value_rows.reshape(SRC, HEADS, HD).transpose(1, 0, 2)
    query_grad, key_grad, value_grad = lax.map(lambda four: head_grads(*four), (query_heads, grad_heads, key_heads, value_heads))
    d_query = query_grad.transpose(1, 0, 2).reshape(TGT, INNER)
    key_low = key_grad.transpose(1, 0, 2).reshape(SRC, INNER).astype(jnp.bfloat16)
    value_low = value_grad.transpose(1, 0, 2).reshape(SRC, INNER).astype(jnp.bfloat16)
    total = jnp.dot(key_low, w_key.T, preferred_element_type=jnp.float32) + jnp.dot(value_low, w_value.T, preferred_element_type=jnp.float32)
    return (d_query, total.astype(jnp.bfloat16))
```

```python
import functools
import math

import jax
import jax.numpy as jnp
from jax import lax
from jax.experimental import pallas as pl
from jax.experimental.pallas import tpu as pltpu
from jax.sharding import PartitionSpec as P

HD = 64
F32 = jnp.float32
BF16 = jnp.bfloat16


def dot(a, b, over_a, over_b):
    return lax.dot_general(
        a, b, (((over_a,), (over_b,)), ((), ())), preferred_element_type=F32
    )


def fold_rows(x, combine):
    return combine(x.reshape(x.shape[0] // 8, 8, x.shape[1]), axis=0)


def attention_kernel(chunk, qg_ref, kv_ref, kt_ref, dq_ref, dkv_ref, s_ref, p_ref, acc_ref):
    step = pl.program_id(1)
    src, tgt = kv_ref.shape[0], qg_ref.shape[0]
    factor = 1.0 / math.sqrt(HD)
    slope = factor * math.log2(math.e)

    @pl.when(step == 0)
    def _():
        acc_ref[...] = jnp.zeros_like(acc_ref)

    qg = qg_ref[...]
    in_query = lax.broadcasted_iota(jnp.int32, qg.shape, 1) < HD
    zero = jnp.zeros_like(qg)
    q_only = jnp.where(in_query, qg, zero)
    g_only = jnp.where(in_query, zero, qg)

    chunks = [pl.ds(at, chunk) for at in range(0, src, chunk)]
    top = None
    for rows in chunks:
        s = dot(kv_ref[rows, :], q_only, 1, 1)
        s_ref[rows, :] = s
        s = fold_rows(s, jnp.max)
        top = s if top is None else jnp.maximum(top, s)
    top = jnp.max(top, axis=0, keepdims=True)

    total = inner = None
    for rows in chunks:
        expo = jnp.exp2((s_ref[rows, :] - top) * slope)
        p = dot(kv_ref[rows, :], g_only, 1, 1)
        s_ref[rows, :] = expo
        p_ref[rows, :] = p
        t, i = fold_rows(expo, jnp.sum), fold_rows(expo * p, jnp.sum)
        total, inner = (t, i) if total is None else (total + t, inner + i)
    inverse = 1.0 / jnp.sum(total, axis=0, keepdims=True)
    delta = jnp.sum(inner, axis=0, keepdims=True) * inverse

    dq = None
    for rows in chunks:
        weights = s_ref[rows, :] * inverse
        grad = (weights * (p_ref[rows, :] - delta)).astype(BF16)
        acc_ref[rows, :] += dot(weights.astype(BF16), g_only, 1, 0) + dot(grad, q_only, 1, 0)
        part = dot(kt_ref[:, rows], grad, 1, 0)
        dq = part if dq is None else dq + part
    dq = (dq * factor).T
    dq_ref[...] = jnp.concatenate([dq[: tgt // 2], dq[tgt // 2 :]], axis=1).astype(BF16)

    @pl.when(step == pl.num_programs(1) - 1)
    def _():
        acc = acc_ref[...]
        in_key = lax.broadcasted_iota(jnp.int32, acc.shape, 1) < HD
        dkv_ref[...] = jnp.where(in_key, acc * factor, acc).astype(BF16)


def attention(qg, kv, block, chunk):
    heads, tgt, wide = qg.shape
    src = kv.shape[1]
    kt = kv[:, :, :HD].transpose(0, 2, 1)
    flops = 5 * 2 * heads * tgt * src * HD
    return pl.pallas_call(
        functools.partial(attention_kernel, chunk),
        grid=(heads, tgt // block),
        in_specs=[
            pl.BlockSpec((None, block, wide), lambda h, i: (h, i, 0)),
            pl.BlockSpec((None, src, wide), lambda h, i: (h, 0, 0)),
            pl.BlockSpec((None, HD, src), lambda h, i: (h, 0, 0)),
        ],
        out_specs=[
            pl.BlockSpec((None, block // 2, wide), lambda h, i: (h, i, 0)),
            pl.BlockSpec((None, src, wide), lambda h, i: (h, 0, 0)),
        ],
        out_shape=[
            jax.ShapeDtypeStruct((heads, tgt // 2, wide), BF16),
            jax.ShapeDtypeStruct((heads, src, wide), BF16),
        ],
        scratch_shapes=[
            pltpu.VMEM((src, block), F32),
            pltpu.VMEM((src, block), F32),
            pltpu.VMEM((src, wide), F32),
        ],
        compiler_params=pltpu.CompilerParams(vmem_limit_bytes=50 * 1024 * 1024),
        cost_estimate=pl.CostEstimate(
            flops=4 * flops, bytes_accessed=4 * heads * (tgt + src) * wide, transcendentals=heads * tgt * src
        ),
    )(qg, kv, kt)


def local(seq, col, memory, query, out_grad, w_key, w_value):
    tgt, width = query.shape
    heads = width // HD
    groups = math.gcd(heads, seq)
    ranges = seq // groups
    each = heads // groups
    same_range = [[r * groups + g for g in range(groups)] for r in range(ranges)]
    same_heads = [[r * groups + g for r in range(ranges)] for g in range(groups)]

    def deal(x):
        return lax.all_to_all(x, "seq", 0, 0, tiled=True, axis_index_groups=same_range)

    def shift(x, by):
        return lax.ppermute(x, "col", [(i, (i + by) % col) for i in range(col)])

    def pair(a, b):
        rows = a.shape[0]
        a, b = a.reshape(rows, heads, HD), b.reshape(rows, heads, HD)
        return jnp.concatenate([a, b], axis=-1).transpose(1, 0, 2)

    own = lax.all_to_all(memory, "seq", split_axis=0, concat_axis=1, tiled=True)
    rows = own.shape[0]
    mem = [own] + [shift(own, by) for by in range(1, col)]

    qg = deal(pair(query, out_grad))
    qg = qg.reshape(groups, each, tgt, 2 * HD).transpose(1, 0, 2, 3).reshape(each, groups * tgt, 2 * HD)

    mem = jnp.concatenate(mem, axis=0)
    total = mem.shape[0]
    kv = pair(dot(mem, w_key, 1, 0).astype(BF16), dot(mem, w_value, 1, 0).astype(BF16))
    kv = deal(kv)
    if ranges > 1:
        kv = lax.all_gather(kv, "seq", axis=0, tiled=True, axis_index_groups=same_heads)
    kv = kv.reshape(seq, each, total, 2 * HD).transpose(1, 0, 2, 3).reshape(each, seq * total, 2 * HD)

    dq, dkv = attention(qg, kv, tgt, 256)

    dq = dq.reshape(each, groups, tgt // 2, 2 * HD).transpose(1, 0, 2, 3)
    dq = deal(dq.reshape(heads, tgt // 2, 2 * HD))
    dq = dq.reshape(heads, tgt // 2, 2, HD).transpose(2, 1, 0, 3).reshape(tgt, width)

    dkv = dkv.reshape(each, seq, total, 2 * HD).transpose(1, 0, 2, 3).reshape(seq * each, total, 2 * HD)
    if ranges > 1:
        dkv = lax.psum_scatter(dkv, "seq", scatter_dimension=0, tiled=True, axis_index_groups=same_heads)
    dkv = deal(dkv).reshape(heads, total, 2, HD).transpose(2, 1, 0, 3).reshape(2, total, width)

    part = dot(dkv[0], w_key, 1, 1) + dot(dkv[1], w_value, 1, 1)
    summed = part[:rows]
    for by in range(1, col):
        summed = summed + shift(part[by * rows : (by + 1) * rows].astype(BF16), col - by).astype(F32)
    d_memory = lax.all_to_all(summed.astype(BF16), "seq", split_axis=1, concat_axis=0, tiled=True)
    return dq, d_memory


def solution(mesh):
    return jax.shard_map(
        functools.partial(local, mesh.shape["seq"], mesh.shape["col"]),
        mesh=mesh,
        in_specs=(
            P("col", "seq"),
            P("seq", "col"),
            P("seq", "col"),
            P(None, "col"),
            P(None, "col"),
        ),
        out_specs=(P("seq", "col"), P("col", "seq")),
        check_vma=False,
    )
```

```python
import functools
import math

import jax
import jax.numpy as jnp
from jax import lax
from jax.experimental import pallas as pl
from jax.experimental.pallas import tpu as pltpu
from jax.sharding import PartitionSpec as P

HD = 64
F32 = jnp.float32
BF16 = jnp.bfloat16
VMEM = pl.BlockSpec(memory_space=pltpu.VMEM)
SMEM = pl.BlockSpec(memory_space=pltpu.SMEM)
MIB = 1024 * 1024


def dot(a, b, over_a, over_b):
    return lax.dot_general(
        a, b, (((over_a,), (over_b,)), ((), ())), preferred_element_type=F32
    )


def whole(kernel, out, *args, after=(), scratch=(), limit=24, flops=0):
    n = len(args)
    moved = sum(x.size * x.dtype.itemsize for x in args)
    return pl.pallas_call(
        lambda *refs: kernel(*refs[:n], *refs[n + len(after) :]),
        in_specs=[SMEM if x.dtype == jnp.int32 else VMEM for x in args]
        + [pl.BlockSpec(memory_space=pl.ANY)] * len(after),
        out_specs=[VMEM] * len(out),
        out_shape=out,
        scratch_shapes=scratch,
        compiler_params=pltpu.CompilerParams(vmem_limit_bytes=limit * MIB),
        cost_estimate=pl.CostEstimate(flops=flops, bytes_accessed=moved, transcendentals=0),
    )(*args, *after)


def head_of(x, h):
    return x[:, h * HD : (h + 1) * HD]


def pair_heads(query, out_grad):
    tgt, width = query.shape

    def kernel(q_ref, g_ref, out_ref):
        for h in range(width // HD):
            cols = pl.ds(h * HD, HD)
            out_ref[h] = jnp.concatenate([q_ref[:, cols], g_ref[:, cols]], axis=1)

    out = [jax.ShapeDtypeStruct((width // HD, tgt, 2 * HD), BF16)]
    return whole(kernel, out, query, out_grad)[0]


def pair_targets(query, out_grad, me, spans):
    tgt, width = query.shape
    place = [(i, at) for i, span in enumerate(spans) for at in range(len(span))]
    out = [
        jax.ShapeDtypeStruct((len(span), 2, tgt, 2 * HD), BF16) for span in spans for _ in range(2)
    ]

    def kernel(me_ref, q_ref, g_ref, *rest):
        out_refs, paired = rest[:-1], rest[-1]
        for h in range(width // HD):
            cols = pl.ds(h * HD, HD)
            paired[h] = jnp.concatenate([q_ref[:, cols], g_ref[:, cols]], axis=1)
        for i, at in place:
            for bits in range(4):
                head = (4 * spans[i][at] + bits) ^ me_ref[0]
                out_refs[2 * i + bits // 2][at, bits % 2] = paired[head]

    scratch = [pltpu.VMEM((width // HD, tgt, 2 * HD), BF16)]
    return whole(kernel, out, me, query, out_grad, scratch=scratch)


def cross(kept, came, after=()):
    def kernel(kept_ref, came_ref, first_ref, second_ref):
        for i, ref in enumerate((kept_ref, came_ref)):
            first_ref[:, i] = ref[:, 0]
            second_ref[:, i] = ref[:, 1]

    out = [jax.ShapeDtypeStruct(kept.shape, kept.dtype)] * 2
    return whole(kernel, out, kept, came, after=after)


def join(kept, came, after=()):
    def kernel(kept_ref, came_ref, *out_refs):
        for d, out_ref in enumerate(out_refs):
            out_ref[0] = kept_ref[d]
            out_ref[1] = came_ref[d]

    out = [jax.ShapeDtypeStruct((2, *kept.shape[1:]), kept.dtype)] * kept.shape[0]
    return whole(kernel, out, kept, came, after=after)


def part_ways(pieces, after=()):
    def kernel(*refs):
        kept_ref, left_ref = refs[-2:]
        for d, ref in enumerate(refs[:-2]):
            kept_ref[d] = ref[0]
            left_ref[d] = ref[1]

    out = [jax.ShapeDtypeStruct((len(pieces), *pieces[0].shape[1:]), pieces[0].dtype)] * 2
    return whole(kernel, out, *pieces, after=after)


def concat(pieces, after=()):
    rows = [x.shape[0] for x in pieces]

    def kernel(*refs):
        at = 0
        for ref, n in zip(refs[:-1], rows):
            refs[-1][at : at + n] = ref[...]
            at += n

    out = [jax.ShapeDtypeStruct((sum(rows), *pieces[0].shape[1:]), pieces[0].dtype)]
    return whole(kernel, out, *pieces, after=after)[0]


def project(mem, w_key, w_value, before=None, after=()):
    blocks, rows, depth = mem.shape
    depth *= blocks
    width = w_key.shape[1]
    heads = width // HD
    tile = math.gcd(width, 256)
    ahead = 0 if before is None else before.shape[1]

    def kernel(m_ref, k_ref, v_ref, *refs):
        out_ref = refs[-1]
        if ahead:
            out_ref[:, :ahead, :] = refs[0][...]
        m = jnp.concatenate([m_ref[b] for b in range(blocks)], axis=1)
        for at in range(0, width, tile):
            key = dot(m, k_ref[:, at : at + tile], 1, 0).astype(BF16)
            value = dot(m, v_ref[:, at : at + tile], 1, 0).astype(BF16)
            for h in range(tile // HD):
                out_ref[at // HD + h, ahead:, :] = jnp.concatenate(
                    [head_of(key, h), head_of(value, h)], axis=1
                )

    out = [jax.ShapeDtypeStruct((heads, ahead + rows, 2 * HD), BF16)]
    args = (mem, w_key, w_value) + (() if before is None else (before,))
    return whole(kernel, out, *args, after=after, flops=4 * rows * depth * width)[0]


def memory_grad(dkv, at, rows, w_key, w_value, blocks, dtype, span=(0, 1), after=()):
    heads = dkv.shape[0]
    depth, width = w_key.shape
    each = depth // blocks
    tile = max(each, math.gcd(depth, 512))
    low, high = (int(depth * x) // tile * tile for x in span)

    def kernel(d_ref, k_ref, v_ref, out_ref):
        d = [d_ref[h, at : at + rows, :] for h in range(heads)]
        dk = jnp.concatenate([x[:, :HD] for x in d], axis=1)
        dv = jnp.concatenate([x[:, HD:] for x in d], axis=1)
        for start in range(low, high, tile):
            here = pl.ds(start, tile)
            part = dot(k_ref[here, :], dk, 1, 1) + dot(v_ref[here, :], dv, 1, 1)
            part = part.T.astype(dtype)
            for b in range(tile // each):
                out_ref[(start - low) // each + b] = part[:, b * each : (b + 1) * each]

    out = [jax.ShapeDtypeStruct(((high - low) // each, rows, each), dtype)]
    flops = 4 * rows * (high - low) * width
    return whole(kernel, out, dkv, w_key, w_value, after=after, flops=flops)[0]


def add_up(parts, others, after=()):
    def kernel(*refs):
        out_ref, at = refs[-1], 0
        for ref in refs[: len(parts)]:
            here = pl.ds(at, ref.shape[0])
            total = ref[...]
            for other in refs[len(parts) : -1]:
                total = total + other[here].astype(F32)
            out_ref[here] = total.astype(BF16)
            at += ref.shape[0]

    out = [jax.ShapeDtypeStruct((sum(x.shape[0] for x in parts), *parts[0].shape[1:]), BF16)]
    return whole(kernel, out, *parts, *others, after=after)[0]


def unpack_query_grad(kept, came, me):
    far, _, half, wide = kept.shape
    heads = 4 * far

    def kernel(me_ref, kept_ref, came_ref, out_ref, by_head):
        for d in range(far):
            for bits in range(4):
                ref = came_ref if bits // 2 else kept_ref
                by_head[(4 * d + bits) ^ me_ref[0]] = ref[d, bits % 2]
        for side in range(2):
            rows = [by_head[h][:, side * HD : (side + 1) * HD] for h in range(heads)]
            out_ref[pl.ds(side * half, half), :] = jnp.concatenate(rows, axis=1)

    out = [jax.ShapeDtypeStruct((2 * half, heads * HD), BF16)]
    return whole(kernel, out, me, kept, came, scratch=[pltpu.VMEM((heads, half, wide), BF16)])[0]


def fold_rows(x, combine):
    return combine(x.reshape(x.shape[0] // 8, 8, x.shape[1]), axis=0)


def attention_kernel(chunk, rows, first, last, qg_ref, kv_ref, *refs):
    step = pl.program_id(1)
    begin = (pl.program_id(0) == 0) & (step == 0)
    end = (pl.program_id(0) == pl.num_programs(0) - 1) & (step == pl.num_programs(1) - 1)
    if not first:
        before_ref, *refs = refs
    if last:
        wk_ref, wv_ref, dq_ref, dkv_ref, wk_out, wv_out, sem, *refs = refs
    else:
        dq_ref, dkv_ref, *refs = refs
    s_ref, p_ref, acc_ref, kt_ref = refs

    fetches = []
    if last:
        fetches.append(pltpu.make_async_copy(wk_ref, wk_out, sem.at[0]))
        fetches.append(pltpu.make_async_copy(wv_ref, wv_out, sem.at[1]))

    @pl.when(begin)
    def _():
        for fetch in fetches:
            fetch.start()

    src, tgt = kv_ref.shape[0], qg_ref.shape[0]
    factor = 1.0 / math.sqrt(HD)
    slope = factor * math.log2(math.e)

    @pl.when(step == 0)
    def _():
        acc_ref[...] = jnp.zeros_like(acc_ref) if first else before_ref[...]
        kt_ref[...] = kv_ref[...].T[:HD]

    qg = qg_ref[...]
    in_query = lax.broadcasted_iota(jnp.int32, qg.shape, 1) < HD
    zero = jnp.zeros_like(qg)
    q_only = jnp.where(in_query, qg, zero)
    g_only = jnp.where(in_query, zero, qg)

    chunks = [pl.ds(at, chunk) for at in range(0, src, chunk)]
    top = None
    for here in chunks:
        s = dot(kv_ref[here, :], q_only, 1, 1)
        s_ref[here, :] = s
        s = fold_rows(s, jnp.max)
        top = s if top is None else jnp.maximum(top, s)
    top = jnp.max(top, axis=0, keepdims=True)

    total = inner = None
    for here in chunks:
        expo = jnp.exp2((s_ref[here, :] - top) * slope)
        p = dot(kv_ref[here, :], g_only, 1, 1)
        s_ref[here, :] = expo
        p_ref[here, :] = p
        t, i = fold_rows(expo, jnp.sum), fold_rows(expo * p, jnp.sum)
        total, inner = (t, i) if total is None else (total + t, inner + i)
    inverse = 1.0 / jnp.sum(total, axis=0, keepdims=True)
    delta = jnp.sum(inner, axis=0, keepdims=True) * inverse

    dq = None
    for here in chunks:
        weights = s_ref[here, :] * inverse
        grad = (weights * (p_ref[here, :] - delta)).astype(BF16)
        acc_ref[here, :] += dot(weights.astype(BF16), g_only, 1, 0) + dot(grad, q_only, 1, 0)
        part = dot(kt_ref[:, here], grad, 1, 0)
        dq = part if dq is None else dq + part
    dq = (dq * factor).T
    half = rows // 2
    for at in range(0, tgt, rows):
        dq_ref[at // 2 : at // 2 + half, :] = jnp.concatenate(
            [dq[at : at + half], dq[at + half : at + rows]], axis=1
        ).astype(BF16)

    @pl.when(step == pl.num_programs(1) - 1)
    def _():
        acc = acc_ref[...]
        if last:
            in_key = lax.broadcasted_iota(jnp.int32, acc.shape, 1) < HD
            acc = jnp.where(in_key, acc * factor, acc)
        dkv_ref[...] = acc.astype(dkv_ref.dtype)

    @pl.when(end)
    def _():
        for fetch in fetches:
            fetch.wait()


def attention(qg, kv, rows, before=None, weights=(), block=512, chunk=256):
    heads, tgt, wide = qg.shape
    src = kv.shape[1]
    first, last = before is None, bool(weights)
    work = heads * tgt * src
    block = max(math.gcd(tgt, block), rows)
    every = pl.BlockSpec((None, src, wide), lambda h, i: (h, 0, 0))
    anywhere = pl.BlockSpec(memory_space=pl.ANY)
    return pl.pallas_call(
        functools.partial(attention_kernel, chunk, rows, first, last),
        grid=(heads, tgt // block),
        in_specs=[pl.BlockSpec((None, block, wide), lambda h, i: (h, i, 0)), every]
        + [every] * (not first)
        + [anywhere] * len(weights),
        out_specs=[pl.BlockSpec((None, block // 2, wide), lambda h, i: (h, i, 0)), every]
        + [anywhere] * len(weights),
        out_shape=[
            jax.ShapeDtypeStruct((heads, tgt // 2, wide), BF16),
            jax.ShapeDtypeStruct((heads, src, wide), BF16 if last else F32),
        ]
        + [pltpu.VMEM(w.shape, w.dtype) for w in weights],
        scratch_shapes=[pltpu.SemaphoreType.DMA((2,))] * last
        + [
            pltpu.VMEM((src, block), F32),
            pltpu.VMEM((src, block), F32),
            pltpu.VMEM((src, wide), F32),
            pltpu.VMEM((HD, src), BF16),
        ],
        compiler_params=pltpu.CompilerParams(vmem_limit_bytes=32 * MIB),
        cost_estimate=pl.CostEstimate(
            flops=5 * 8 * work * HD, bytes_accessed=8 * heads * (tgt + src) * wide, transcendentals=work
        ),
    )(qg, kv, *(() if first else (before,)), *weights)


def local(seq, col, memory, query, out_grad, w_key, w_value):
    tgt, width = query.shape
    heads = width // HD
    groups = math.gcd(heads, seq)
    ranges = seq // groups
    each = heads // groups
    same_range = [[r * groups + g for g in range(groups)] for r in range(ranges)]
    same_heads = [[r * groups + g for r in range(ranges)] for g in range(groups)]
    pairwise = ranges == 1 and each == 1 and groups >= 16 and groups & (groups - 1) == 0
    me = lax.axis_index("seq").astype(jnp.int32) if pairwise else jnp.int32(0)
    me = me.reshape(1)
    far = groups // 4

    def deal(x):
        return lax.all_to_all(x, "seq", 0, 0, tiled=True, axis_index_groups=same_range)

    def swap(x, bits):
        return lax.ppermute(x, "seq", [(i, i ^ bits) for i in range(seq)])

    def gather_far(x, d):
        return swap(x, 4 * d) if d else x

    def by_head(x, many):
        x = x.reshape(many, each, *x.shape[1:]).swapaxes(0, 1)
        return x.reshape(each, many * x.shape[2], x.shape[3])

    def by_owner(x, many):
        x = x.reshape(each, many, x.shape[1] // many, x.shape[2]).swapaxes(0, 1)
        return x.reshape(many * each, *x.shape[2:])

    def shift(x, by):
        return lax.ppermute(x, "col", [(i, (i + by) % col) for i in range(col)])

    rows = memory.shape[0] // seq
    total = rows * col
    own = lax.all_to_all(memory.reshape(seq, rows, -1), "seq", 0, 0, tiled=True)

    if pairwise:
        early = far // 2
        late = [d for d in range(far) if d != early]
        kept, left, kept_late, left_late = pair_targets(query, out_grad, me, [[early], late])
        kept, left = cross(kept, swap(left, 2))
        early_qg, own = lax.optimization_barrier((join(kept, swap(left, 1))[0], own))
        early_qg = gather_far(early_qg, early)
        left_late = concat([left_late], after=(own,))
        left_late = swap(left_late, 2)
        kv = project(own, w_key, w_value)
        kept, left = cross(kept_late, left_late, after=(kv, early_qg))
        late_qg = join(kept, swap(left, 1))
        for by in range(1, col):
            kv = project(shift(own, by), w_key, w_value, kv, after=(early_qg, late_qg[0]))
        kv = deal(kv)
        late_qg = [gather_far(x, d) for x, d in zip(late_qg, late)]
        qg = [[late_qg[0], early_qg], late_qg[1:]]
        order = [0, early, *late[1:]]
    else:
        qg = deal(pair_heads(query, out_grad))
        kv = project(own, w_key, w_value)
        for by in range(1, col):
            kv = project(shift(own, by), w_key, w_value, kv)
        kv = deal(kv)
        qg = [by_head(qg, groups)]
    if ranges > 1:
        kv = lax.all_gather(kv, "seq", axis=0, tiled=True, axis_index_groups=same_heads)
    kv = by_head(kv, seq)

    dq, dkv = [], None
    for i, x in enumerate(qg):
        if pairwise:
            x = concat([piece.reshape(-1, 2 * HD) for piece in x], after=(dkv,) * (i > 0))[None]
        weights = (w_key, w_value) if i == len(qg) - 1 else ()
        part, dkv, *weights = attention(x, kv, tgt, dkv, weights)
        dq.append(part)
    w_key, w_value = weights
    dkv = by_owner(dkv, seq)
    if ranges > 1:
        dkv = lax.psum_scatter(dkv, "seq", scatter_dimension=0, tiled=True, axis_index_groups=same_heads)
    dkv = deal(dkv)

    others = [memory_grad(dkv, by * rows, rows, w_key, w_value, seq, BF16) for by in range(1, col)]
    others = [shift(x, col - 1 - i) for i, x in enumerate(others)]
    mine = [memory_grad(dkv, 0, rows, w_key, w_value, seq, F32, (0, 0.25))]
    mine.append(memory_grad(dkv, 0, rows, w_key, w_value, seq, F32, (0.25, 1)))
    if pairwise:
        dq = concat([x.reshape(-1, 2, 2, tgt // 2, 2 * HD) for x in dq], after=mine[:1])
        dq = [gather_far(dq[order.index(d)], d) for d in range(far)]
        summed = add_up(mine, others, after=dq)
        kept, left = part_ways(dq, after=(summed,))
        kept, left = cross(kept, swap(left, 1))
        dq = unpack_query_grad(kept, swap(left, 2), me)
    else:
        summed = add_up(mine, others)
        dq = deal(by_owner(dq[0], groups))
        dq = dq.reshape(heads, tgt // 2, 2, HD).transpose(2, 1, 0, 3).reshape(tgt, width)
    d_memory = lax.all_to_all(summed, "seq", 0, 0, tiled=True)
    return dq, d_memory.reshape(memory.shape)


def solution(mesh):
    return jax.shard_map(
        functools.partial(local, mesh.shape["seq"], mesh.shape["col"]),
        mesh=mesh,
        in_specs=(
            P("col", "seq"),
            P("seq", "col"),
            P("seq", "col"),
            P(None, "col"),
            P(None, "col"),
        ),
        out_specs=(P("seq", "col"), P("col", "seq")),
        check_vma=False,
    )
```

```python
import functools
import math

import jax
import jax.numpy as jnp
from jax import lax
from jax.experimental import pallas as pl
from jax.experimental.pallas import tpu as pltpu
from jax.sharding import PartitionSpec as P

HD = 64
F32 = jnp.float32
BF16 = jnp.bfloat16
VMEM = pl.BlockSpec(memory_space=pltpu.VMEM)
SMEM = pl.BlockSpec(memory_space=pltpu.SMEM)
MIB = 1024 * 1024


def dot(a, b, over_a, over_b):
    return lax.dot_general(
        a, b, (((over_a,), (over_b,)), ((), ())), preferred_element_type=F32
    )


def whole(kernel, out, *args, after=(), scratch=(), limit=16, flops=0):
    n = len(args)
    moved = sum(x.size * x.dtype.itemsize for x in args)
    return pl.pallas_call(
        lambda *refs: kernel(*refs[:n], *refs[n + len(after) :]),
        in_specs=[SMEM if x.dtype == jnp.int32 else VMEM for x in args]
        + [pl.BlockSpec(memory_space=pl.ANY)] * len(after),
        out_specs=[VMEM] * len(out),
        out_shape=out,
        scratch_shapes=scratch,
        compiler_params=pltpu.CompilerParams(vmem_limit_bytes=limit * MIB),
        cost_estimate=pl.CostEstimate(flops=flops, bytes_accessed=moved, transcendentals=0),
    )(*args, *after)


def head_of(x, h):
    return x[:, h * HD : (h + 1) * HD]


def pair_heads(query, out_grad):
    tgt, width = query.shape

    def kernel(q_ref, g_ref, out_ref):
        for h in range(width // HD):
            cols = pl.ds(h * HD, HD)
            out_ref[h] = jnp.concatenate([q_ref[:, cols], g_ref[:, cols]], axis=1)

    out = [jax.ShapeDtypeStruct((width // HD, tgt, 2 * HD), BF16)]
    return whole(kernel, out, query, out_grad)[0]


def pair_targets(query, out_grad, me, spans):
    tgt, width = query.shape
    place = [(i, at) for i, span in enumerate(spans) for at in range(len(span))]
    out = [
        jax.ShapeDtypeStruct((len(span), 2, tgt, 2 * HD), BF16) for span in spans for _ in range(2)
    ]

    def kernel(me_ref, q_ref, g_ref, *rest):
        out_refs, paired = rest[:-1], rest[-1]
        for h in range(width // HD):
            cols = pl.ds(h * HD, HD)
            paired[h] = jnp.concatenate([q_ref[:, cols], g_ref[:, cols]], axis=1)
        for i, at in place:
            for bits in range(4):
                head = (4 * spans[i][at] + bits) ^ me_ref[0]
                out_refs[2 * i + bits // 2][at, bits % 2] = paired[head]

    scratch = [pltpu.VMEM((width // HD, tgt, 2 * HD), BF16)]
    return whole(kernel, out, me, query, out_grad, scratch=scratch)


def cross(kept, came, after=()):
    n = kept.shape[0]

    def kernel(kept_ref, came_ref, first_ref, *second_refs):
        for i, ref in enumerate((kept_ref, came_ref)):
            first_ref[:, i] = ref[:, 0]
            for d, second_ref in enumerate(second_refs):
                second_ref[i] = ref[d, 1]

    out = [jax.ShapeDtypeStruct(kept.shape, kept.dtype)] + [jax.ShapeDtypeStruct(kept.shape[1:], kept.dtype)] * n
    first, *second = whole(kernel, out, kept, came, after=after)
    return first, second


def join(kept, came, after=()):
    def kernel(kept_ref, *refs):
        for d in range(len(came)):
            out_ref = refs[len(came) + d]
            out_ref[0] = kept_ref[d]
            out_ref[1] = refs[d][...]

    out = [jax.ShapeDtypeStruct((2, *kept.shape[1:]), kept.dtype)] * kept.shape[0]
    return whole(kernel, out, kept, *came, after=after)


def part_ways(pieces, after=()):
    def kernel(*refs):
        kept_ref, left_ref = refs[-2:]
        for d, ref in enumerate(refs[:-2]):
            kept_ref[d] = ref[0]
            left_ref[d] = ref[1]

    out = [jax.ShapeDtypeStruct((len(pieces), *pieces[0].shape[1:]), pieces[0].dtype)] * 2
    return whole(kernel, out, *pieces, after=after)


def concat(pieces, after=()):
    rows = [x.shape[0] for x in pieces]

    def kernel(*refs):
        at = 0
        for ref, n in zip(refs[:-1], rows):
            refs[-1][at : at + n] = ref[...]
            at += n

    out = [jax.ShapeDtypeStruct((sum(rows), *pieces[0].shape[1:]), pieces[0].dtype)]
    return whole(kernel, out, *pieces, after=after)[0]


def project(mem, w_key, w_value, before=None, after=()):
    blocks, rows, depth = mem.shape
    depth *= blocks
    width = w_key.shape[1]
    heads = width // HD
    tile = math.gcd(width, 256)
    ahead = 0 if before is None else before.shape[1]

    def kernel(m_ref, k_ref, v_ref, *refs):
        out_ref = refs[-1]
        if ahead:
            out_ref[:, :ahead, :] = refs[0][...]
        m = jnp.concatenate([m_ref[b] for b in range(blocks)], axis=1)
        for at in range(0, width, tile):
            key = dot(m, k_ref[:, at : at + tile], 1, 0).astype(BF16)
            value = dot(m, v_ref[:, at : at + tile], 1, 0).astype(BF16)
            for h in range(tile // HD):
                out_ref[at // HD + h, ahead:, :] = jnp.concatenate(
                    [head_of(key, h), head_of(value, h)], axis=1
                )

    out = [jax.ShapeDtypeStruct((heads, ahead + rows, 2 * HD), BF16)]
    args = (mem, w_key, w_value) + (() if before is None else (before,))
    return whole(kernel, out, *args, after=after, flops=4 * rows * depth * width)[0]


def memory_grad(dkv, at, rows, w_key, w_value, blocks, dtype, span=(0, 1), after=()):
    heads = dkv.shape[0]
    depth, width = w_key.shape
    each = depth // blocks
    tile = max(each, math.gcd(depth, 512))
    low, high = (int(depth * x) // tile * tile for x in span)

    def kernel(d_ref, k_ref, v_ref, out_ref):
        d = [d_ref[h, at : at + rows, :] for h in range(heads)]
        dk = jnp.concatenate([x[:, :HD] for x in d], axis=1)
        dv = jnp.concatenate([x[:, HD:] for x in d], axis=1)
        for start in range(low, high, tile):
            here = pl.ds(start, tile)
            part = dot(k_ref[here, :], dk, 1, 1) + dot(v_ref[here, :], dv, 1, 1)
            part = part.T.astype(dtype)
            for b in range(tile // each):
                out_ref[(start - low) // each + b] = part[:, b * each : (b + 1) * each]

    out = [jax.ShapeDtypeStruct(((high - low) // each, rows, each), dtype)]
    flops = 4 * rows * (high - low) * width
    return whole(kernel, out, dkv, w_key, w_value, after=after, flops=flops)[0]


def project_and_fetch(mem, w_key, w_value):
    blocks, rows, each = mem.shape
    depth, width = w_key.shape
    heads = width // HD
    steps = math.gcd(blocks, 8)
    tall, per = depth // steps, blocks // steps

    def kernel(m_ref, k_hbm, v_hbm, out_ref, k_ref, v_ref, key_ref, value_ref, sem):
        copies = []
        for i in range(steps):
            here = pl.ds(i * tall, tall)
            copies.append(
                [
                    pltpu.make_async_copy(k_hbm.at[here], k_ref.at[here], sem.at[0, i]),
                    pltpu.make_async_copy(v_hbm.at[here], v_ref.at[here], sem.at[1, i]),
                ]
            )
        for pair in copies:
            for copy in pair:
                copy.start()
        for i, pair in enumerate(copies):
            here = pl.ds(i * tall, tall)
            m = jnp.concatenate([m_ref[b] for b in range(i * per, (i + 1) * per)], axis=1)
            for copy, ref, sum_ref in zip(pair, (k_ref, v_ref), (key_ref, value_ref)):
                copy.wait()
                part = dot(m, ref[here, :], 1, 0)
                sum_ref[...] = part if i == 0 else sum_ref[...] + part
        key, value = key_ref[...].astype(BF16), value_ref[...].astype(BF16)
        for h in range(heads):
            out_ref[h] = jnp.concatenate([head_of(key, h), head_of(value, h)], axis=1)

    anywhere = pl.BlockSpec(memory_space=pl.ANY)
    return pl.pallas_call(
        kernel,
        in_specs=[VMEM, anywhere, anywhere],
        out_specs=[VMEM] * 3,
        out_shape=[
            jax.ShapeDtypeStruct((heads, rows, 2 * HD), BF16),
            pltpu.VMEM(w_key.shape, BF16),
            pltpu.VMEM(w_value.shape, BF16),
        ],
        scratch_shapes=[
            pltpu.VMEM((rows, width), F32),
            pltpu.VMEM((rows, width), F32),
            pltpu.SemaphoreType.DMA((2, steps)),
        ],
        compiler_params=pltpu.CompilerParams(vmem_limit_bytes=12 * MIB),
        cost_estimate=pl.CostEstimate(
            flops=4 * rows * depth * width, bytes_accessed=4 * depth * width, transcendentals=0
        ),
    )(mem, *[pltpu.with_memory_space_constraint(w, pltpu.MemorySpace.HBM) for w in (w_key, w_value)])


def add_up(parts, others, after=()):
    def kernel(*refs):
        out_ref, at = refs[-1], 0
        for ref in refs[: len(parts)]:
            here = pl.ds(at, ref.shape[0])
            total = ref[...]
            for other in refs[len(parts) : -1]:
                total = total + other[here].astype(F32)
            out_ref[here] = total.astype(BF16)
            at += ref.shape[0]

    out = [jax.ShapeDtypeStruct((sum(x.shape[0] for x in parts), *parts[0].shape[1:]), BF16)]
    return whole(kernel, out, *parts, *others, after=after)[0]


def unpack_query_grad(kept, came, me):
    far, _, half, wide = kept.shape
    heads = 4 * far

    def kernel(me_ref, kept_ref, came_ref, out_ref, by_head):
        for d in range(far):
            for bits in range(4):
                ref = came_ref if bits // 2 else kept_ref
                by_head[(4 * d + bits) ^ me_ref[0]] = ref[d, bits % 2]
        for side in range(2):
            rows = [by_head[h][:, side * HD : (side + 1) * HD] for h in range(heads)]
            out_ref[pl.ds(side * half, half), :] = jnp.concatenate(rows, axis=1)

    out = [jax.ShapeDtypeStruct((2 * half, heads * HD), BF16)]
    return whole(kernel, out, me, kept, came, scratch=[pltpu.VMEM((heads, half, wide), BF16)])[0]


def fold_rows(x, combine):
    return combine(x.reshape(x.shape[0] // 8, 8, x.shape[1]), axis=0)


def attention_kernel(tile, chunk, rows, first, last, qg_ref, kv_ref, *refs):
    step = pl.program_id(1)
    begin = (pl.program_id(0) == 0) & (step == 0)
    end = (pl.program_id(0) == pl.num_programs(0) - 1) & (step == pl.num_programs(1) - 1)
    if not first:
        before_ref, *refs = refs
    if last:
        wk_ref, wv_ref, dq_ref, dkv_ref, wk_out, wv_out, sem, *refs = refs
    else:
        dq_ref, dkv_ref, *refs = refs
    s_ref, e_ref, p_ref, acc_ref, kt_ref = refs

    fetches = []
    if last:
        fetches.append(pltpu.make_async_copy(wk_ref, wk_out, sem.at[0]))
        fetches.append(pltpu.make_async_copy(wv_ref, wv_out, sem.at[1]))

    @pl.when(begin)
    def _():
        for fetch in fetches:
            fetch.start()

    src, tgt = kv_ref.shape[0], qg_ref.shape[0]
    factor = 1.0 / math.sqrt(HD)
    slope = factor * math.log2(math.e)

    @pl.when(step == 0)
    def _():
        acc_ref[...] = jnp.zeros_like(acc_ref) if first else before_ref[...]
        kt_ref[...] = kv_ref[...].T[:HD]

    chunks = [pl.ds(at, chunk) for at in range(0, src, chunk)]
    tiles = tgt // tile
    q_only, g_only, both = {}, {}, {}
    last_top = inverse = delta = None
    for t in range(tiles + 2):
        if t < tiles:
            qg = qg_ref[pl.ds(t * tile, tile), :]
            in_query = lax.broadcasted_iota(jnp.int32, qg.shape, 1) < HD
            zero = jnp.zeros_like(qg)
            q_only[t] = jnp.where(in_query, qg, zero)
            g_only[t] = jnp.where(in_query, zero, qg)
            both[t] = jnp.concatenate([g_only[t], q_only[t]], axis=0)
        top = total = inner = dq = None
        for here in chunks:
            if t >= 2:
                weights = e_ref[here, :] * inverse
                grad = (weights * (p_ref[here, :] - delta)).astype(BF16)
                pair = jnp.concatenate([weights.astype(BF16), grad], axis=1)
                acc_ref[here, :] += dot(pair, both[t - 2], 1, 0)
                part = dot(kt_ref[:, here], grad, 1, 0)
                dq = part if dq is None else dq + part
            if 1 <= t <= tiles:
                expo = jnp.exp2((s_ref[here, :] - last_top) * slope)
                p = dot(kv_ref[here, :], g_only[t - 1], 1, 1)
                e_ref[here, :] = expo
                p_ref[here, :] = p
                sums = fold_rows(expo, jnp.sum), fold_rows(expo * p, jnp.sum)
                total, inner = sums if total is None else (total + sums[0], inner + sums[1])
            if t < tiles:
                s = dot(kv_ref[here, :], q_only[t], 1, 1)
                s_ref[here, :] = s
                s = fold_rows(s, jnp.max)
                top = s if top is None else jnp.maximum(top, s)
        if t >= 2:
            dq = (dq * factor).T
            half = rows // 2
            for at in range(0, tile, rows):
                to = ((t - 2) * tile + at) // 2
                dq_ref[to : to + half, :] = jnp.concatenate(
                    [dq[at : at + half], dq[at + half : at + rows]], axis=1
                ).astype(BF16)
        if 1 <= t <= tiles:
            inverse = 1.0 / jnp.sum(total, axis=0, keepdims=True)
            delta = jnp.sum(inner, axis=0, keepdims=True) * inverse
        if t < tiles:
            last_top = jnp.max(top, axis=0, keepdims=True)

    @pl.when(step == pl.num_programs(1) - 1)
    def _():
        acc = acc_ref[...]
        if last:
            in_key = lax.broadcasted_iota(jnp.int32, acc.shape, 1) < HD
            acc = jnp.where(in_key, acc * factor, acc)
        dkv_ref[...] = acc.astype(dkv_ref.dtype)

    @pl.when(end)
    def _():
        for fetch in fetches:
            fetch.wait()


def attention(qg, kv, rows, before=None, weights=(), block=2048, tile=256, chunk=512):
    heads, tgt, wide = qg.shape
    src = kv.shape[1]
    first, last = before is None, bool(weights)
    work = heads * tgt * src
    tile = max(math.gcd(tgt, tile), rows)
    block = max(math.gcd(tgt, block), tile)
    weights = [pltpu.with_memory_space_constraint(w, pltpu.MemorySpace.HBM) for w in weights]
    every = pl.BlockSpec((None, src, wide), lambda h, i: (h, 0, 0))
    anywhere = pl.BlockSpec(memory_space=pl.ANY)
    return pl.pallas_call(
        functools.partial(attention_kernel, tile, math.gcd(src, chunk), rows, first, last),
        grid=(heads, tgt // block),
        in_specs=[pl.BlockSpec((None, block, wide), lambda h, i: (h, i, 0)), every]
        + [every] * (not first)
        + [anywhere] * len(weights),
        out_specs=[pl.BlockSpec((None, block // 2, wide), lambda h, i: (h, i, 0)), every]
        + [anywhere] * len(weights),
        out_shape=[
            jax.ShapeDtypeStruct((heads, tgt // 2, wide), BF16),
            jax.ShapeDtypeStruct((heads, src, wide), BF16 if last else F32),
        ]
        + [pltpu.VMEM(w.shape, w.dtype) for w in weights],
        scratch_shapes=[pltpu.SemaphoreType.DMA((2,))] * last
        + [
            pltpu.VMEM((src, tile), F32),
            pltpu.VMEM((src, tile), F32),
            pltpu.VMEM((src, tile), F32),
            pltpu.VMEM((src, wide), F32),
            pltpu.VMEM((HD, src), BF16),
        ],
        compiler_params=pltpu.CompilerParams(vmem_limit_bytes=32 * MIB),
        cost_estimate=pl.CostEstimate(
            flops=5 * 8 * work * HD, bytes_accessed=8 * heads * (tgt + src) * wide, transcendentals=work
        ),
    )(qg, kv, *(() if first else (before,)), *weights)


def local(seq, col, memory, query, out_grad, w_key, w_value):
    tgt, width = query.shape
    heads = width // HD
    groups = math.gcd(heads, seq)
    ranges = seq // groups
    each = heads // groups
    same_range = [[r * groups + g for g in range(groups)] for r in range(ranges)]
    same_heads = [[r * groups + g for r in range(ranges)] for g in range(groups)]
    pairwise = ranges == 1 and each == 1 and groups >= 16 and groups & (groups - 1) == 0
    me = lax.axis_index("seq").astype(jnp.int32) if pairwise else jnp.int32(0)
    me = me.reshape(1)
    far = groups // 4

    def deal(x):
        return lax.all_to_all(x, "seq", 0, 0, tiled=True, axis_index_groups=same_range)

    def swap(x, bits):
        return lax.ppermute(x, "seq", [(i, i ^ bits) for i in range(seq)])

    def gather_far(x, d):
        return swap(x, 4 * d) if d else x

    def by_head(x, many):
        x = x.reshape(many, each, *x.shape[1:]).swapaxes(0, 1)
        return x.reshape(each, many * x.shape[2], x.shape[3])

    def by_owner(x, many):
        x = x.reshape(each, many, x.shape[1] // many, x.shape[2]).swapaxes(0, 1)
        return x.reshape(many * each, *x.shape[2:])

    def shift(x, by):
        return lax.ppermute(x, "col", [(i, (i + by) % col) for i in range(col)])

    rows = memory.shape[0] // seq
    total = rows * col
    own = lax.all_to_all(memory.reshape(seq, rows, -1), "seq", 0, 0, tiled=True)

    if pairwise:
        early = far // 2
        late = [d for d in range(far) if d != early]
        kept, left, kept_late, left_late = pair_targets(query, out_grad, me, [[early], late])
        kept, left = cross(kept, swap(left, 2))
        early_qg, own = lax.optimization_barrier((join(kept, [swap(x, 1) for x in left])[0], own))
        early_qg = gather_far(early_qg, early)
        left_late = concat([left_late], after=(own,))
        left_late = swap(left_late, 2)
        kv, *held = project_and_fetch(own, w_key, w_value)
        kept, left = cross(kept_late, left_late, after=(kv,))
        late_qg = join(kept, [swap(x, 1) for x in left])
        for by in range(1, col):
            kv = project(shift(own, by), *held, kv, after=(early_qg, late_qg[0]))
        kv = deal(kv)
        late_qg = [gather_far(x, d) for x, d in zip(late_qg, late)]
        qg = [[late_qg[0], early_qg], late_qg[1:]]
        order = [0, early, *late[1:]]
    else:
        qg = deal(pair_heads(query, out_grad))
        kv = project(own, w_key, w_value)
        for by in range(1, col):
            kv = project(shift(own, by), w_key, w_value, kv)
        kv = deal(kv)
        qg = [by_head(qg, groups)]
    if ranges > 1:
        kv = lax.all_gather(kv, "seq", axis=0, tiled=True, axis_index_groups=same_heads)
    kv = by_head(kv, seq)

    dq, dkv = [], None
    for i, x in enumerate(qg):
        if pairwise:
            x = concat([piece.reshape(-1, 2 * HD) for piece in x], after=(dkv,) * (i > 0))[None]
        weights = (w_key, w_value) if i == len(qg) - 1 else ()
        part, dkv, *weights = attention(x, kv, tgt, dkv, weights)
        dq.append(part)
    w_key, w_value = weights
    dkv = by_owner(dkv, seq)
    if ranges > 1:
        dkv = lax.psum_scatter(dkv, "seq", scatter_dimension=0, tiled=True, axis_index_groups=same_heads)
    dkv = deal(dkv)

    others = [memory_grad(dkv, by * rows, rows, w_key, w_value, seq, BF16) for by in range(1, col)]
    others = [shift(x, col - 1 - i) for i, x in enumerate(others)]
    mine = [memory_grad(dkv, 0, rows, w_key, w_value, seq, F32, (0, 0.125))]
    mine.append(memory_grad(dkv, 0, rows, w_key, w_value, seq, F32, (0.125, 1)))
    if pairwise:
        dq = concat([x.reshape(-1, 2, 2, tgt // 2, 2 * HD) for x in dq], after=mine[:1])
        dq = [gather_far(dq[order.index(d)], d) for d in range(far)]
        summed = add_up(mine, others, after=dq)
        kept, left = part_ways(dq, after=(summed,))
        kept, left = cross(kept, swap(left, 1))
        dq = unpack_query_grad(kept, swap(concat([x[None] for x in left]), 2), me)
    else:
        summed = add_up(mine, others)
        dq = deal(by_owner(dq[0], groups))
        dq = dq.reshape(heads, tgt // 2, 2, HD).transpose(2, 1, 0, 3).reshape(tgt, width)
    d_memory = lax.all_to_all(summed, "seq", 0, 0, tiled=True)
    return dq, d_memory.reshape(memory.shape)


def solution(mesh):
    return jax.shard_map(
        functools.partial(local, mesh.shape["seq"], mesh.shape["col"]),
        mesh=mesh,
        in_specs=(
            P("col", "seq"),
            P("seq", "col"),
            P("seq", "col"),
            P(None, "col"),
            P(None, "col"),
        ),
        out_specs=(P("seq", "col"), P("col", "seq")),
        check_vma=False,
    )
```

```python
import functools
import math

import jax
import jax.numpy as jnp
from jax import lax
from jax.experimental import pallas as pl
from jax.experimental.pallas import tpu as pltpu
from jax.sharding import PartitionSpec as P

HD = 64
F32 = jnp.float32
BF16 = jnp.bfloat16
VMEM = pl.BlockSpec(memory_space=pltpu.VMEM)
SMEM = pl.BlockSpec(memory_space=pltpu.SMEM)
MIB = 1024 * 1024


def dot(a, b, over_a, over_b):
    return lax.dot_general(
        a, b, (((over_a,), (over_b,)), ((), ())), preferred_element_type=F32
    )


def whole(kernel, out, *args, after=(), scratch=(), limit=16, flops=0):
    n = len(args)
    moved = sum(x.size * x.dtype.itemsize for x in args)
    return pl.pallas_call(
        lambda *refs: kernel(*refs[:n], *refs[n + len(after) :]),
        in_specs=[SMEM if x.dtype == jnp.int32 else VMEM for x in args]
        + [pl.BlockSpec(memory_space=pl.ANY)] * len(after),
        out_specs=[VMEM] * len(out),
        out_shape=out,
        scratch_shapes=scratch,
        compiler_params=pltpu.CompilerParams(vmem_limit_bytes=limit * MIB),
        cost_estimate=pl.CostEstimate(flops=flops, bytes_accessed=moved, transcendentals=0),
    )(*args, *after)


def head_of(x, h):
    return x[:, h * HD : (h + 1) * HD]


def pair_heads(query, out_grad):
    tgt, width = query.shape

    def kernel(q_ref, g_ref, out_ref):
        for h in range(width // HD):
            cols = pl.ds(h * HD, HD)
            out_ref[h] = jnp.concatenate([q_ref[:, cols], g_ref[:, cols]], axis=1)

    out = [jax.ShapeDtypeStruct((width // HD, tgt, 2 * HD), BF16)]
    return whole(kernel, out, query, out_grad)[0]


def pair_targets(query, out_grad, me, spans):
    tgt, width = query.shape
    place = [(i, at) for i, span in enumerate(spans) for at in range(len(span))]
    out = [
        jax.ShapeDtypeStruct((len(span), 2, tgt, 2 * HD), BF16) for span in spans for _ in range(2)
    ]

    def kernel(me_ref, q_ref, g_ref, *rest):
        out_refs, paired = rest[:-1], rest[-1]
        for h in range(width // HD):
            cols = pl.ds(h * HD, HD)
            paired[h] = jnp.concatenate([q_ref[:, cols], g_ref[:, cols]], axis=1)
        for i, at in place:
            for bits in range(4):
                head = (4 * spans[i][at] + bits) ^ me_ref[0]
                out_refs[2 * i + bits // 2][at, bits % 2] = paired[head]

    scratch = [pltpu.VMEM((width // HD, tgt, 2 * HD), BF16)]
    return whole(kernel, out, me, query, out_grad, scratch=scratch)


def cross(kept, came, after=()):
    n = kept.shape[0]

    def kernel(kept_ref, came_ref, first_ref, *second_refs):
        for i, ref in enumerate((kept_ref, came_ref)):
            first_ref[:, i] = ref[:, 0]
            for d, second_ref in enumerate(second_refs):
                second_ref[i] = ref[d, 1]

    out = [jax.ShapeDtypeStruct(kept.shape, kept.dtype)] + [jax.ShapeDtypeStruct(kept.shape[1:], kept.dtype)] * n
    first, *second = whole(kernel, out, kept, came, after=after)
    return first, second


def join(kept, came, after=()):
    def kernel(kept_ref, *refs):
        for d in range(len(came)):
            out_ref = refs[len(came) + d]
            out_ref[0] = kept_ref[d]
            out_ref[1] = refs[d][...]

    out = [jax.ShapeDtypeStruct((2, *kept.shape[1:]), kept.dtype)] * kept.shape[0]
    return whole(kernel, out, kept, *came, after=after)


def part_ways(pieces, after=()):
    def kernel(*refs):
        kept_ref, left_ref = refs[-2:]
        for d, ref in enumerate(refs[:-2]):
            kept_ref[d] = ref[0]
            left_ref[d] = ref[1]

    out = [jax.ShapeDtypeStruct((len(pieces), *pieces[0].shape[1:]), pieces[0].dtype)] * 2
    return whole(kernel, out, *pieces, after=after)


def concat(pieces, after=()):
    rows = [x.shape[0] for x in pieces]

    def kernel(*refs):
        at = 0
        for ref, n in zip(refs[:-1], rows):
            refs[-1][at : at + n] = ref[...]
            at += n

    out = [jax.ShapeDtypeStruct((sum(rows), *pieces[0].shape[1:]), pieces[0].dtype)]
    return whole(kernel, out, *pieces, after=after)[0]


def project(mem, w_key, w_value, before=None, after=()):
    blocks, rows, depth = mem.shape
    depth *= blocks
    width = w_key.shape[1]
    heads = width // HD
    tile = math.gcd(width, 256)
    ahead = 0 if before is None else before.shape[1]

    def kernel(m_ref, k_ref, v_ref, *refs):
        out_ref = refs[-1]
        if ahead:
            out_ref[:, :ahead, :] = refs[0][...]
        m = jnp.concatenate([m_ref[b] for b in range(blocks)], axis=1)
        for at in range(0, width, tile):
            key = dot(m, k_ref[:, at : at + tile], 1, 0).astype(BF16)
            value = dot(m, v_ref[:, at : at + tile], 1, 0).astype(BF16)
            for h in range(tile // HD):
                out_ref[at // HD + h, ahead:, :] = jnp.concatenate(
                    [head_of(key, h), head_of(value, h)], axis=1
                )

    out = [jax.ShapeDtypeStruct((heads, ahead + rows, 2 * HD), BF16)]
    args = (mem, w_key, w_value) + (() if before is None else (before,))
    return whole(kernel, out, *args, after=after, flops=4 * rows * depth * width)[0]


def memory_grad(dkv, at, rows, w_key, w_value, blocks, dtype, span=(0, 1), after=()):
    heads = dkv.shape[0]
    depth, width = w_key.shape
    each = depth // blocks
    tile = max(each, math.gcd(depth, 512))
    low, high = (int(depth * x) // tile * tile for x in span)

    def kernel(d_ref, k_ref, v_ref, out_ref):
        d = [d_ref[h, at : at + rows, :] for h in range(heads)]
        dk = jnp.concatenate([x[:, :HD] for x in d], axis=1)
        dv = jnp.concatenate([x[:, HD:] for x in d], axis=1)
        for start in range(low, high, tile):
            here = pl.ds(start, tile)
            part = dot(k_ref[here, :], dk, 1, 1) + dot(v_ref[here, :], dv, 1, 1)
            part = part.T.astype(dtype)
            for b in range(tile // each):
                out_ref[(start - low) // each + b] = part[:, b * each : (b + 1) * each]

    out = [jax.ShapeDtypeStruct(((high - low) // each, rows, each), dtype)]
    flops = 4 * rows * (high - low) * width
    return whole(kernel, out, dkv, w_key, w_value, after=after, flops=flops)[0]


def project_and_fetch(mem, w_key, w_value):
    blocks, rows, each = mem.shape
    depth, width = w_key.shape
    heads = width // HD
    steps = math.gcd(blocks, 8)
    tall, per = depth // steps, blocks // steps

    def kernel(m_ref, k_hbm, v_hbm, out_ref, k_ref, v_ref, key_ref, value_ref, sem):
        copies = []
        for i in range(steps):
            here = pl.ds(i * tall, tall)
            copies.append(
                [
                    pltpu.make_async_copy(k_hbm.at[here], k_ref.at[here], sem.at[0, i]),
                    pltpu.make_async_copy(v_hbm.at[here], v_ref.at[here], sem.at[1, i]),
                ]
            )
        for pair in copies:
            for copy in pair:
                copy.start()
        for i, pair in enumerate(copies):
            here = pl.ds(i * tall, tall)
            m = jnp.concatenate([m_ref[b] for b in range(i * per, (i + 1) * per)], axis=1)
            for copy, ref, sum_ref in zip(pair, (k_ref, v_ref), (key_ref, value_ref)):
                copy.wait()
                part = dot(m, ref[here, :], 1, 0)
                sum_ref[...] = part if i == 0 else sum_ref[...] + part
        key, value = key_ref[...].astype(BF16), value_ref[...].astype(BF16)
        for h in range(heads):
            out_ref[h] = jnp.concatenate([head_of(key, h), head_of(value, h)], axis=1)

    anywhere = pl.BlockSpec(memory_space=pl.ANY)
    return pl.pallas_call(
        kernel,
        in_specs=[VMEM, anywhere, anywhere],
        out_specs=[VMEM] * 3,
        out_shape=[
            jax.ShapeDtypeStruct((heads, rows, 2 * HD), BF16),
            pltpu.VMEM(w_key.shape, BF16),
            pltpu.VMEM(w_value.shape, BF16),
        ],
        scratch_shapes=[
            pltpu.VMEM((rows, width), F32),
            pltpu.VMEM((rows, width), F32),
            pltpu.SemaphoreType.DMA((2, steps)),
        ],
        compiler_params=pltpu.CompilerParams(vmem_limit_bytes=12 * MIB),
        cost_estimate=pl.CostEstimate(
            flops=4 * rows * depth * width, bytes_accessed=4 * depth * width, transcendentals=0
        ),
    )(mem, *[pltpu.with_memory_space_constraint(w, pltpu.MemorySpace.HBM) for w in (w_key, w_value)])


def add_up(parts, others, after=()):
    def kernel(*refs):
        out_ref, at = refs[-1], 0
        for ref in refs[: len(parts)]:
            here = pl.ds(at, ref.shape[0])
            total = ref[...]
            for other in refs[len(parts) : -1]:
                total = total + other[here].astype(F32)
            out_ref[here] = total.astype(BF16)
            at += ref.shape[0]

    out = [jax.ShapeDtypeStruct((sum(x.shape[0] for x in parts), *parts[0].shape[1:]), BF16)]
    return whole(kernel, out, *parts, *others, after=after)[0]


def unpack_query_grad(kept, came, me):
    far, _, half, wide = kept.shape
    heads = 4 * far

    def kernel(me_ref, kept_ref, came_ref, out_ref, by_head):
        for d in range(far):
            for bits in range(4):
                ref = came_ref if bits // 2 else kept_ref
                by_head[(4 * d + bits) ^ me_ref[0]] = ref[d, bits % 2]
        for side in range(2):
            rows = [by_head[h][:, side * HD : (side + 1) * HD] for h in range(heads)]
            out_ref[pl.ds(side * half, half), :] = jnp.concatenate(rows, axis=1)

    out = [jax.ShapeDtypeStruct((2 * half, heads * HD), BF16)]
    return whole(kernel, out, me, kept, came, scratch=[pltpu.VMEM((heads, half, wide), BF16)])[0]


def fold_rows(x, combine):
    return combine(x.reshape(x.shape[0] // 8, 8, x.shape[1]), axis=0)


def attention_kernel(tile, chunk, rows, first, last, qg_ref, kv_ref, *refs):
    step = pl.program_id(1)
    begin = (pl.program_id(0) == 0) & (step == 0)
    end = (pl.program_id(0) == pl.num_programs(0) - 1) & (step == pl.num_programs(1) - 1)
    if not first:
        before_ref, *refs = refs
    if last:
        wk_ref, wv_ref, dq_ref, dkv_ref, wk_out, wv_out, sem, *refs = refs
    else:
        dq_ref, dkv_ref, *refs = refs
    s_ref, e_ref, p_ref, acc_ref, kt_ref = refs

    fetches = []
    if last:
        fetches.append(pltpu.make_async_copy(wk_ref, wk_out, sem.at[0]))
        fetches.append(pltpu.make_async_copy(wv_ref, wv_out, sem.at[1]))

    @pl.when(begin)
    def _():
        for fetch in fetches:
            fetch.start()

    src, tgt = kv_ref.shape[0], qg_ref.shape[0]
    factor = 1.0 / math.sqrt(HD)
    slope = factor * math.log2(math.e)

    @pl.when(step == 0)
    def _():
        acc_ref[...] = jnp.zeros_like(acc_ref) if first else before_ref[...]
        kt_ref[...] = kv_ref[...].T[:HD]

    chunks = [pl.ds(at, chunk) for at in range(0, src, chunk)]
    tiles = tgt // tile

    def load(t):
        qg = qg_ref[pl.ds(pl.multiple_of(t * tile, tile), tile), :]
        in_query = lax.broadcasted_iota(jnp.int32, qg.shape, 1) < HD
        zero = jnp.zeros_like(qg)
        return jnp.where(in_query, qg, zero), jnp.where(in_query, zero, qg)

    def advance(t, carry, scores=True, weigh=True, grads=True):
        last_top, inverse, delta = carry
        top = total = inner = dq = None
        if scores:
            q_only, _ = load(t)
        if weigh:
            _, g_last = load(t - 1)
        if grads:
            q, g = load(t - 2)
            both = jnp.concatenate([g, q], axis=0)
        for here in chunks:
            if grads:
                weights = e_ref[here, :] * inverse
                grad = (weights * (p_ref[here, :] - delta)).astype(BF16)
                pair = jnp.concatenate([weights.astype(BF16), grad], axis=1)
                acc_ref[here, :] += dot(pair, both, 1, 0)
                part = dot(kt_ref[:, here], grad, 1, 0)
                dq = part if dq is None else dq + part
            if weigh:
                expo = jnp.exp2((s_ref[here, :] - last_top) * slope)
                p = dot(kv_ref[here, :], g_last, 1, 1)
                e_ref[here, :] = expo
                p_ref[here, :] = p
                sums = fold_rows(expo, jnp.sum), fold_rows(expo * p, jnp.sum)
                total, inner = sums if total is None else (total + sums[0], inner + sums[1])
            if scores:
                s = dot(kv_ref[here, :], q_only, 1, 1)
                s_ref[here, :] = s
                s = fold_rows(s, jnp.max)
                top = s if top is None else jnp.maximum(top, s)
        if grads:
            dq = (dq * factor).T
            half = rows // 2
            for at in range(0, tile, rows):
                to = pl.multiple_of((t - 2) * (tile // 2) + at // 2, half)
                dq_ref[pl.ds(to, half), :] = jnp.concatenate(
                    [dq[at : at + half], dq[at + half : at + rows]], axis=1
                ).astype(BF16)
        if weigh:
            inverse = 1.0 / jnp.sum(total, axis=0, keepdims=True)
            delta = jnp.sum(inner, axis=0, keepdims=True) * inverse
        if scores:
            last_top = jnp.max(top, axis=0, keepdims=True)
        return last_top, inverse, delta

    nothing = jnp.zeros((1, tile), F32)
    carry = advance(0, (nothing,) * 3, weigh=False, grads=False)
    if tiles > 1:
        carry = advance(1, carry, grads=False)
        carry = lax.fori_loop(2, tiles, advance, carry)
    carry = advance(tiles, carry, scores=False, grads=tiles > 1)
    advance(tiles + 1, carry, scores=False, weigh=False)

    @pl.when(step == pl.num_programs(1) - 1)
    def _():
        acc = acc_ref[...]
        if last:
            in_key = lax.broadcasted_iota(jnp.int32, acc.shape, 1) < HD
            acc = jnp.where(in_key, acc * factor, acc)
        dkv_ref[...] = acc.astype(dkv_ref.dtype)

    @pl.when(end)
    def _():
        for fetch in fetches:
            fetch.wait()


def attention(qg, kv, rows, before=None, weights=(), block=2048, tile=256, chunk=512):
    heads, tgt, wide = qg.shape
    src = kv.shape[1]
    first, last = before is None, bool(weights)
    work = heads * tgt * src
    tile = max(math.gcd(tgt, tile), rows)
    block = max(math.gcd(tgt, block), tile)
    weights = [pltpu.with_memory_space_constraint(w, pltpu.MemorySpace.HBM) for w in weights]
    every = pl.BlockSpec((None, src, wide), lambda h, i: (h, 0, 0))
    anywhere = pl.BlockSpec(memory_space=pl.ANY)
    return pl.pallas_call(
        functools.partial(attention_kernel, tile, math.gcd(src, chunk), rows, first, last),
        grid=(heads, tgt // block),
        in_specs=[pl.BlockSpec((None, block, wide), lambda h, i: (h, i, 0)), every]
        + [every] * (not first)
        + [anywhere] * len(weights),
        out_specs=[pl.BlockSpec((None, block // 2, wide), lambda h, i: (h, i, 0)), every]
        + [anywhere] * len(weights),
        out_shape=[
            jax.ShapeDtypeStruct((heads, tgt // 2, wide), BF16),
            jax.ShapeDtypeStruct((heads, src, wide), BF16 if last else F32),
        ]
        + [pltpu.VMEM(w.shape, w.dtype) for w in weights],
        scratch_shapes=[pltpu.SemaphoreType.DMA((2,))] * last
        + [
            pltpu.VMEM((src, tile), F32),
            pltpu.VMEM((src, tile), F32),
            pltpu.VMEM((src, tile), F32),
            pltpu.VMEM((src, wide), F32),
            pltpu.VMEM((HD, src), BF16),
        ],
        compiler_params=pltpu.CompilerParams(vmem_limit_bytes=32 * MIB),
        cost_estimate=pl.CostEstimate(
            flops=5 * 8 * work * HD, bytes_accessed=8 * heads * (tgt + src) * wide, transcendentals=work
        ),
    )(qg, kv, *(() if first else (before,)), *weights)


def local(seq, col, memory, query, out_grad, w_key, w_value):
    tgt, width = query.shape
    heads = width // HD
    groups = math.gcd(heads, seq)
    ranges = seq // groups
    each = heads // groups
    same_range = [[r * groups + g for g in range(groups)] for r in range(ranges)]
    same_heads = [[r * groups + g for r in range(ranges)] for g in range(groups)]
    pairwise = ranges == 1 and each == 1 and groups >= 16 and groups & (groups - 1) == 0
    me = lax.axis_index("seq").astype(jnp.int32) if pairwise else jnp.int32(0)
    me = me.reshape(1)
    far = groups // 4

    def deal(x):
        return lax.all_to_all(x, "seq", 0, 0, tiled=True, axis_index_groups=same_range)

    def swap(x, bits):
        return lax.ppermute(x, "seq", [(i, i ^ bits) for i in range(seq)])

    def gather_far(x, d):
        return swap(x, 4 * d) if d else x

    def by_head(x, many):
        x = x.reshape(many, each, *x.shape[1:]).swapaxes(0, 1)
        return x.reshape(each, many * x.shape[2], x.shape[3])

    def by_owner(x, many):
        x = x.reshape(each, many, x.shape[1] // many, x.shape[2]).swapaxes(0, 1)
        return x.reshape(many * each, *x.shape[2:])

    def shift(x, by):
        return lax.ppermute(x, "col", [(i, (i + by) % col) for i in range(col)])

    rows = memory.shape[0] // seq
    total = rows * col
    own = lax.all_to_all(memory.reshape(seq, rows, -1), "seq", 0, 0, tiled=True)

    if pairwise:
        early = far // 2
        late = [d for d in range(far) if d != early]
        kept, left, kept_late, left_late = pair_targets(query, out_grad, me, [[early], late])
        kept, left = cross(kept, swap(left, 2))
        early_qg, own = lax.optimization_barrier((join(kept, [swap(x, 1) for x in left])[0], own))
        early_qg = gather_far(early_qg, early)
        left_late = concat([left_late], after=(own,))
        left_late = swap(left_late, 2)
        kv, *held = project_and_fetch(own, w_key, w_value)
        kept, left = cross(kept_late, left_late, after=(kv,))
        late_qg = join(kept, [swap(x, 1) for x in left])
        for by in range(1, col):
            kv = project(shift(own, by), *held, kv, after=(early_qg, late_qg[0]))
        kv = deal(kv)
        late_qg = [gather_far(x, d) for x, d in zip(late_qg, late)]
        qg = [[late_qg[0], early_qg], late_qg[1:]]
        order = [0, early, *late[1:]]
    else:
        qg = deal(pair_heads(query, out_grad))
        kv = project(own, w_key, w_value)
        for by in range(1, col):
            kv = project(shift(own, by), w_key, w_value, kv)
        kv = deal(kv)
        qg = [by_head(qg, groups)]
    if ranges > 1:
        kv = lax.all_gather(kv, "seq", axis=0, tiled=True, axis_index_groups=same_heads)
    kv = by_head(kv, seq)

    dq, dkv = [], None
    for i, x in enumerate(qg):
        if pairwise:
            x = concat([piece.reshape(-1, 2 * HD) for piece in x], after=(dkv,) * (i > 0))[None]
        weights = (w_key, w_value) if i == len(qg) - 1 else ()
        part, dkv, *weights = attention(x, kv, tgt, dkv, weights)
        dq.append(part)
    w_key, w_value = weights
    dkv = by_owner(dkv, seq)
    if ranges > 1:
        dkv = lax.psum_scatter(dkv, "seq", scatter_dimension=0, tiled=True, axis_index_groups=same_heads)
    dkv = deal(dkv)

    others = [memory_grad(dkv, by * rows, rows, w_key, w_value, seq, BF16) for by in range(1, col)]
    others = [shift(x, col - 1 - i) for i, x in enumerate(others)]
    mine = [memory_grad(dkv, 0, rows, w_key, w_value, seq, F32, (0, 0.125))]
    mine.append(memory_grad(dkv, 0, rows, w_key, w_value, seq, F32, (0.125, 1)))
    if pairwise:
        dq = concat([x.reshape(-1, 2, 2, tgt // 2, 2 * HD) for x in dq], after=mine[:1])
        dq = [gather_far(dq[order.index(d)], d) for d in range(far)]
        summed = add_up(mine, others, after=dq)
        kept, left = part_ways(dq, after=(summed,))
        kept, left = cross(kept, swap(left, 1))
        dq = unpack_query_grad(kept, swap(concat([x[None] for x in left]), 2), me)
    else:
        summed = add_up(mine, others)
        dq = deal(by_owner(dq[0], groups))
        dq = dq.reshape(heads, tgt // 2, 2, HD).transpose(2, 1, 0, 3).reshape(tgt, width)
    d_memory = lax.all_to_all(summed, "seq", 0, 0, tiled=True)
    return dq, d_memory.reshape(memory.shape)


def solution(mesh):
    return jax.shard_map(
        functools.partial(local, mesh.shape["seq"], mesh.shape["col"]),
        mesh=mesh,
        in_specs=(
            P("col", "seq"),
            P("seq", "col"),
            P("seq", "col"),
            P(None, "col"),
            P(None, "col"),
        ),
        out_specs=(P("seq", "col"), P("col", "seq")),
        check_vma=False,
    )
```

```python
import functools
import math

import jax
import jax.numpy as jnp
from jax import lax
from jax.experimental import pallas as pl
from jax.experimental.pallas import tpu as pltpu
from jax.sharding import PartitionSpec as P

HD = 64
F32 = jnp.float32
BF16 = jnp.bfloat16
VMEM = pl.BlockSpec(memory_space=pltpu.VMEM)
SMEM = pl.BlockSpec(memory_space=pltpu.SMEM)
MIB = 1024 * 1024


def dot(a, b, over_a, over_b):
    return lax.dot_general(
        a, b, (((over_a,), (over_b,)), ((), ())), preferred_element_type=F32
    )


def whole(kernel, out, *args, after=(), scratch=(), limit=16, flops=0):
    n = len(args)
    moved = sum(x.size * x.dtype.itemsize for x in args)
    return pl.pallas_call(
        lambda *refs: kernel(*refs[:n], *refs[n + len(after) :]),
        in_specs=[SMEM if x.dtype == jnp.int32 else VMEM for x in args]
        + [pl.BlockSpec(memory_space=pl.ANY)] * len(after),
        out_specs=[VMEM] * len(out),
        out_shape=out,
        scratch_shapes=scratch,
        compiler_params=pltpu.CompilerParams(vmem_limit_bytes=limit * MIB),
        cost_estimate=pl.CostEstimate(flops=flops, bytes_accessed=moved, transcendentals=0),
    )(*args, *after)


def head_of(x, h):
    return x[:, h * HD : (h + 1) * HD]


def pair_heads(query, out_grad):
    tgt, width = query.shape

    def kernel(q_ref, g_ref, out_ref):
        for h in range(width // HD):
            cols = pl.ds(h * HD, HD)
            out_ref[h] = jnp.concatenate([q_ref[:, cols], g_ref[:, cols]], axis=1)

    out = [jax.ShapeDtypeStruct((width // HD, tgt, 2 * HD), BF16)]
    return whole(kernel, out, query, out_grad)[0]


def pair_targets(query, out_grad, me, spans):
    tgt, width = query.shape
    place = [(i, at) for i, span in enumerate(spans) for at in range(len(span))]
    out = [
        jax.ShapeDtypeStruct((len(span), 2, tgt, 2 * HD), BF16) for span in spans for _ in range(2)
    ]

    def kernel(me_ref, q_ref, g_ref, *rest):
        out_refs, paired = rest[:-1], rest[-1]
        for h in range(width // HD):
            cols = pl.ds(h * HD, HD)
            paired[h] = jnp.concatenate([q_ref[:, cols], g_ref[:, cols]], axis=1)
        for i, at in place:
            for bits in range(4):
                head = (4 * spans[i][at] + bits) ^ me_ref[0]
                out_refs[2 * i + bits // 2][at, bits % 2] = paired[head]

    scratch = [pltpu.VMEM((width // HD, tgt, 2 * HD), BF16)]
    return whole(kernel, out, me, query, out_grad, scratch=scratch)


def cross(kept, came, after=()):
    n = kept.shape[0]

    def kernel(kept_ref, came_ref, first_ref, *second_refs):
        for i, ref in enumerate((kept_ref, came_ref)):
            first_ref[:, i] = ref[:, 0]
            for d, second_ref in enumerate(second_refs):
                second_ref[i] = ref[d, 1]

    out = [jax.ShapeDtypeStruct(kept.shape, kept.dtype)] + [jax.ShapeDtypeStruct(kept.shape[1:], kept.dtype)] * n
    first, *second = whole(kernel, out, kept, came, after=after)
    return first, second


def join(kept, came, after=()):
    def kernel(kept_ref, *refs):
        for d in range(len(came)):
            out_ref = refs[len(came) + d]
            out_ref[0] = kept_ref[d]
            out_ref[1] = refs[d][...]

    out = [jax.ShapeDtypeStruct((2, *kept.shape[1:]), kept.dtype)] * kept.shape[0]
    return whole(kernel, out, kept, *came, after=after)


def part_ways(pieces, after=()):
    def kernel(*refs):
        kept_ref, left_ref = refs[-2:]
        for d, ref in enumerate(refs[:-2]):
            kept_ref[d] = ref[0]
            left_ref[d] = ref[1]

    out = [jax.ShapeDtypeStruct((len(pieces), *pieces[0].shape[1:]), pieces[0].dtype)] * 2
    return whole(kernel, out, *pieces, after=after)


def concat(pieces, after=()):
    rows = [x.shape[0] for x in pieces]

    def kernel(*refs):
        at = 0
        for ref, n in zip(refs[:-1], rows):
            refs[-1][at : at + n] = ref[...]
            at += n

    out = [jax.ShapeDtypeStruct((sum(rows), *pieces[0].shape[1:]), pieces[0].dtype)]
    return whole(kernel, out, *pieces, after=after)[0]


def project(mem, w_key, w_value, before=None, after=()):
    blocks, rows, depth = mem.shape
    depth *= blocks
    width = w_key.shape[1]
    heads = width // HD
    tile = math.gcd(width, 256)
    ahead = 0 if before is None else before.shape[1]

    def kernel(m_ref, k_ref, v_ref, *refs):
        out_ref = refs[-1]
        if ahead:
            out_ref[:, :ahead, :] = refs[0][...]
        m = jnp.concatenate([m_ref[b] for b in range(blocks)], axis=1)
        for at in range(0, width, tile):
            key = dot(m, k_ref[:, at : at + tile], 1, 0).astype(BF16)
            value = dot(m, v_ref[:, at : at + tile], 1, 0).astype(BF16)
            for h in range(tile // HD):
                out_ref[at // HD + h, ahead:, :] = jnp.concatenate(
                    [head_of(key, h), head_of(value, h)], axis=1
                )

    out = [jax.ShapeDtypeStruct((heads, ahead + rows, 2 * HD), BF16)]
    args = (mem, w_key, w_value) + (() if before is None else (before,))
    return whole(kernel, out, *args, after=after, flops=4 * rows * depth * width)[0]


def memory_grad(dkv, at, rows, w_key, w_value, blocks, dtype, span=(0, 1), after=()):
    heads = dkv.shape[0]
    depth, width = w_key.shape
    each = depth // blocks
    tile = max(each, math.gcd(depth, 512))
    low, high = (int(depth * x) // tile * tile for x in span)

    def kernel(d_ref, k_ref, v_ref, out_ref):
        d = [d_ref[h, at : at + rows, :] for h in range(heads)]
        dk = jnp.concatenate([x[:, :HD] for x in d], axis=1)
        dv = jnp.concatenate([x[:, HD:] for x in d], axis=1)
        for start in range(low, high, tile):
            here = pl.ds(start, tile)
            part = dot(k_ref[here, :], dk, 1, 1) + dot(v_ref[here, :], dv, 1, 1)
            part = part.T.astype(dtype)
            for b in range(tile // each):
                out_ref[(start - low) // each + b] = part[:, b * each : (b + 1) * each]

    out = [jax.ShapeDtypeStruct(((high - low) // each, rows, each), dtype)]
    flops = 4 * rows * (high - low) * width
    return whole(kernel, out, dkv, w_key, w_value, after=after, flops=flops)[0]


def project_and_fetch(mem, w_key, w_value):
    blocks, rows, each = mem.shape
    depth, width = w_key.shape
    heads = width // HD
    steps = math.gcd(blocks, 8)
    tall, per = depth // steps, blocks // steps

    def kernel(m_ref, k_hbm, v_hbm, out_ref, k_ref, v_ref, key_ref, value_ref, sem):
        copies = []
        for i in range(steps):
            here = pl.ds(i * tall, tall)
            copies.append(
                [
                    pltpu.make_async_copy(k_hbm.at[here], k_ref.at[here], sem.at[0, i]),
                    pltpu.make_async_copy(v_hbm.at[here], v_ref.at[here], sem.at[1, i]),
                ]
            )
        for pair in copies:
            for copy in pair:
                copy.start()
        for i, pair in enumerate(copies):
            here = pl.ds(i * tall, tall)
            m = jnp.concatenate([m_ref[b] for b in range(i * per, (i + 1) * per)], axis=1)
            for copy, ref, sum_ref in zip(pair, (k_ref, v_ref), (key_ref, value_ref)):
                copy.wait()
                part = dot(m, ref[here, :], 1, 0)
                sum_ref[...] = part if i == 0 else sum_ref[...] + part
        key, value = key_ref[...].astype(BF16), value_ref[...].astype(BF16)
        for h in range(heads):
            out_ref[h] = jnp.concatenate([head_of(key, h), head_of(value, h)], axis=1)

    anywhere = pl.BlockSpec(memory_space=pl.ANY)
    return pl.pallas_call(
        kernel,
        in_specs=[VMEM, anywhere, anywhere],
        out_specs=[VMEM] * 3,
        out_shape=[
            jax.ShapeDtypeStruct((heads, rows, 2 * HD), BF16),
            pltpu.VMEM(w_key.shape, BF16),
            pltpu.VMEM(w_value.shape, BF16),
        ],
        scratch_shapes=[
            pltpu.VMEM((rows, width), F32),
            pltpu.VMEM((rows, width), F32),
            pltpu.SemaphoreType.DMA((2, steps)),
        ],
        compiler_params=pltpu.CompilerParams(vmem_limit_bytes=12 * MIB),
        cost_estimate=pl.CostEstimate(
            flops=4 * rows * depth * width, bytes_accessed=4 * depth * width, transcendentals=0
        ),
    )(mem, *[pltpu.with_memory_space_constraint(w, pltpu.MemorySpace.HBM) for w in (w_key, w_value)])


def add_up(mine, others, after=()):
    half = mine.shape[0] // 2

    def kernel(mine_ref, *refs):
        out_ref = refs[-1]
        for i in range(2):
            here = pl.ds(i * half, half)
            total = mine_ref[here]
            for ref in refs[i:-1:2]:
                total = total + ref[...].astype(F32)
            out_ref[here] = total.astype(BF16)

    out = [jax.ShapeDtypeStruct(mine.shape, BF16)]
    return whole(kernel, out, mine, *others, after=after)[0]


def unpack_query_grad(kept, came, me):
    far, _, half, wide = kept.shape
    heads = 4 * far

    def kernel(me_ref, kept_ref, came_ref, out_ref, by_head):
        for d in range(far):
            for bits in range(4):
                ref = came_ref if bits // 2 else kept_ref
                by_head[(4 * d + bits) ^ me_ref[0]] = ref[d, bits % 2]
        for side in range(2):
            rows = [by_head[h][:, side * HD : (side + 1) * HD] for h in range(heads)]
            out_ref[pl.ds(side * half, half), :] = jnp.concatenate(rows, axis=1)

    out = [jax.ShapeDtypeStruct((2 * half, heads * HD), BF16)]
    return whole(kernel, out, me, kept, came, scratch=[pltpu.VMEM((heads, half, wide), BF16)])[0]


def fold_rows(x, combine):
    return combine(x.reshape(x.shape[0] // 8, 8, x.shape[1]), axis=0)


def attention_kernel(tile, chunk, rows, first, last, qg_ref, kv_ref, *refs):
    step = pl.program_id(1)
    begin = (pl.program_id(0) == 0) & (step == 0)
    end = (pl.program_id(0) == pl.num_programs(0) - 1) & (step == pl.num_programs(1) - 1)
    if not first:
        before_ref, *refs = refs
    if last:
        wk_ref, wv_ref, dq_ref, dkv_ref, wk_out, wv_out, sem, *refs = refs
    else:
        dq_ref, dkv_ref, *refs = refs
    s_ref, e_ref, p_ref, acc_ref, kt_ref = refs

    fetches = []
    if last:
        fetches.append(pltpu.make_async_copy(wk_ref, wk_out, sem.at[0]))
        fetches.append(pltpu.make_async_copy(wv_ref, wv_out, sem.at[1]))

    @pl.when(begin)
    def _():
        for fetch in fetches:
            fetch.start()

    src, tgt = kv_ref.shape[0], qg_ref.shape[0]
    factor = 1.0 / math.sqrt(HD)
    slope = factor * math.log2(math.e)

    @pl.when(step == 0)
    def _():
        acc_ref[...] = jnp.zeros_like(acc_ref) if first else before_ref[...]
        kt_ref[...] = kv_ref[...].T[:HD]

    chunks = [pl.ds(at, chunk) for at in range(0, src, chunk)]
    tiles = tgt // tile

    def load(t):
        qg = qg_ref[pl.ds(pl.multiple_of(t * tile, tile), tile), :]
        in_query = lax.broadcasted_iota(jnp.int32, qg.shape, 1) < HD
        zero = jnp.zeros_like(qg)
        return jnp.where(in_query, qg, zero), jnp.where(in_query, zero, qg)

    def advance(t, carry, scores=True, weigh=True, grads=True):
        last_top, inverse, delta = carry
        top = total = inner = dq = None
        if scores:
            q_only, _ = load(t)
        if weigh:
            _, g_last = load(t - 1)
        if grads:
            q, g = load(t - 2)
            both = jnp.concatenate([g, q], axis=0)
        for here in chunks:
            if grads:
                weights = e_ref[here, :] * inverse
                grad = (weights * (p_ref[here, :] - delta)).astype(BF16)
                pair = jnp.concatenate([weights.astype(BF16), grad], axis=1)
                acc_ref[here, :] += dot(pair, both, 1, 0)
                part = dot(kt_ref[:, here], grad, 1, 0)
                dq = part if dq is None else dq + part
            if weigh:
                expo = jnp.exp2((s_ref[here, :] - last_top) * slope)
                p = dot(kv_ref[here, :], g_last, 1, 1)
                e_ref[here, :] = expo
                p_ref[here, :] = p
                sums = fold_rows(expo, jnp.sum), fold_rows(expo * p, jnp.sum)
                total, inner = sums if total is None else (total + sums[0], inner + sums[1])
            if scores:
                s = dot(kv_ref[here, :], q_only, 1, 1)
                s_ref[here, :] = s
                s = fold_rows(s, jnp.max)
                top = s if top is None else jnp.maximum(top, s)
        if grads:
            dq = (dq * factor).T
            half = rows // 2
            for at in range(0, tile, rows):
                to = pl.multiple_of((t - 2) * (tile // 2) + at // 2, half)
                dq_ref[pl.ds(to, half), :] = jnp.concatenate(
                    [dq[at : at + half], dq[at + half : at + rows]], axis=1
                ).astype(BF16)
        if weigh:
            inverse = 1.0 / jnp.sum(total, axis=0, keepdims=True)
            delta = jnp.sum(inner, axis=0, keepdims=True) * inverse
        if scores:
            last_top = jnp.max(top, axis=0, keepdims=True)
        return last_top, inverse, delta

    nothing = jnp.zeros((1, tile), F32)
    carry = advance(0, (nothing,) * 3, weigh=False, grads=False)
    if tiles > 1:
        carry = advance(1, carry, grads=False)
        carry = lax.fori_loop(2, tiles, advance, carry)
    carry = advance(tiles, carry, scores=False, grads=tiles > 1)
    advance(tiles + 1, carry, scores=False, weigh=False)

    @pl.when(step == pl.num_programs(1) - 1)
    def _():
        acc = acc_ref[...]
        if last:
            in_key = lax.broadcasted_iota(jnp.int32, acc.shape, 1) < HD
            acc = jnp.where(in_key, acc * factor, acc)
        dkv_ref[...] = acc.astype(dkv_ref.dtype)

    @pl.when(end)
    def _():
        for fetch in fetches:
            fetch.wait()


def attention(qg, kv, rows, before=None, weights=(), block=2048, tile=256, chunk=512):
    heads, tgt, wide = qg.shape
    src = kv.shape[1]
    first, last = before is None, bool(weights)
    work = heads * tgt * src
    tile = max(math.gcd(tgt, tile), rows)
    block = max(math.gcd(tgt, block), tile)
    weights = [pltpu.with_memory_space_constraint(w, pltpu.MemorySpace.HBM) for w in weights]
    every = pl.BlockSpec((None, src, wide), lambda h, i: (h, 0, 0))
    anywhere = pl.BlockSpec(memory_space=pl.ANY)
    return pl.pallas_call(
        functools.partial(attention_kernel, tile, math.gcd(src, chunk), rows, first, last),
        grid=(heads, tgt // block),
        in_specs=[pl.BlockSpec((None, block, wide), lambda h, i: (h, i, 0)), every]
        + [every] * (not first)
        + [anywhere] * len(weights),
        out_specs=[pl.BlockSpec((None, block // 2, wide), lambda h, i: (h, i, 0)), every]
        + [anywhere] * len(weights),
        out_shape=[
            jax.ShapeDtypeStruct((heads, tgt // 2, wide), BF16),
            jax.ShapeDtypeStruct((heads, src, wide), BF16 if last else F32),
        ]
        + [pltpu.VMEM(w.shape, w.dtype) for w in weights],
        scratch_shapes=[pltpu.SemaphoreType.DMA((2,))] * last
        + [
            pltpu.VMEM((src, tile), F32),
            pltpu.VMEM((src, tile), F32),
            pltpu.VMEM((src, tile), F32),
            pltpu.VMEM((src, wide), F32),
            pltpu.VMEM((HD, src), BF16),
        ],
        compiler_params=pltpu.CompilerParams(vmem_limit_bytes=32 * MIB),
        cost_estimate=pl.CostEstimate(
            flops=5 * 8 * work * HD, bytes_accessed=8 * heads * (tgt + src) * wide, transcendentals=work
        ),
    )(qg, kv, *(() if first else (before,)), *weights)


def local(seq, col, memory, query, out_grad, w_key, w_value):
    tgt, width = query.shape
    heads = width // HD
    groups = math.gcd(heads, seq)
    ranges = seq // groups
    each = heads // groups
    same_range = [[r * groups + g for g in range(groups)] for r in range(ranges)]
    same_heads = [[r * groups + g for r in range(ranges)] for g in range(groups)]
    pairwise = ranges == 1 and each == 1 and groups >= 16 and groups & (groups - 1) == 0
    me = lax.axis_index("seq").astype(jnp.int32) if pairwise else jnp.int32(0)
    me = me.reshape(1)
    far = groups // 4

    def deal(x):
        return lax.all_to_all(x, "seq", 0, 0, tiled=True, axis_index_groups=same_range)

    def swap(x, bits):
        return lax.ppermute(x, "seq", [(i, i ^ bits) for i in range(seq)])

    def gather_far(x, d):
        return swap(x, 4 * d) if d else x

    def by_head(x, many):
        x = x.reshape(many, each, *x.shape[1:]).swapaxes(0, 1)
        return x.reshape(each, many * x.shape[2], x.shape[3])

    def by_owner(x, many):
        x = x.reshape(each, many, x.shape[1] // many, x.shape[2]).swapaxes(0, 1)
        return x.reshape(many * each, *x.shape[2:])

    def shift(x, by):
        return lax.ppermute(x, "col", [(i, (i + by) % col) for i in range(col)])

    rows = memory.shape[0] // seq
    total = rows * col
    own = lax.all_to_all(memory.reshape(seq, rows, -1), "seq", 0, 0, tiled=True)

    if pairwise:
        early = far // 2
        late = [d for d in range(far) if d != early]
        kept, left, kept_late, left_late = pair_targets(query, out_grad, me, [[early], late])
        kept, left = cross(kept, swap(left, 2))
        early_qg, own = lax.optimization_barrier((join(kept, [swap(x, 1) for x in left])[0], own))
        early_qg = gather_far(early_qg, early)
        left_late = concat([left_late], after=(own,))
        left_late = swap(left_late, 2)
        kv, *held = project_and_fetch(own, w_key, w_value)
        kept, left = cross(kept_late, left_late, after=(kv,))
        late_qg = join(kept, [swap(x, 1) for x in left])
        for by in range(1, col):
            kv = project(shift(own, by), *held, kv, after=(late_qg[0],))
        early_qg, kv = lax.optimization_barrier((early_qg, kv))
        kv = deal(kv)
        late_qg = [gather_far(x, d) for x, d in zip(late_qg, late)]
        qg = [[late_qg[0], early_qg], late_qg[1:]]
    else:
        qg = deal(pair_heads(query, out_grad))
        kv = project(own, w_key, w_value)
        for by in range(1, col):
            kv = project(shift(own, by), w_key, w_value, kv)
        kv = deal(kv)
        qg = [by_head(qg, groups)]
    if ranges > 1:
        kv = lax.all_gather(kv, "seq", axis=0, tiled=True, axis_index_groups=same_heads)
    kv = by_head(kv, seq)

    dq, dkv = [], None
    for i, x in enumerate(qg):
        if pairwise:
            x = concat([piece.reshape(-1, 2 * HD) for piece in x], after=(dkv,) * (i > 0))[None]
        weights = (w_key, w_value) if i == len(qg) - 1 else ()
        part, dkv, *weights = attention(x, kv, tgt, dkv, weights)
        dq.append(part)
        if pairwise and i == 0:
            home, away = dq.pop().reshape(2, 2, 2, tgt // 2, 2 * HD)
            away = gather_far(away, early)
    w_key, w_value = weights
    if pairwise:
        dkv, away = lax.optimization_barrier((dkv, away))
    dkv = by_owner(dkv, seq)
    if ranges > 1:
        dkv = lax.psum_scatter(dkv, "seq", scatter_dimension=0, tiled=True, axis_index_groups=same_heads)
    dkv = deal(dkv)

    others = [
        (by, memory_grad(dkv, by * rows, rows, w_key, w_value, seq, BF16, span))
        for by in range(1, col)
        for span in ((0, 0.5), (0.5, 1))
    ]
    first = [x for _, x in others]
    others = [shift(x, col - by) for by, x in others]
    mine = memory_grad(dkv, 0, rows, w_key, w_value, seq, F32)
    if pairwise:
        dq = concat([x.reshape(-1, 2, 2, tgt // 2, 2 * HD) for x in dq], after=first)
        dq = [home, *[gather_far(x, d) for x, d in zip(dq, late[1:])]]
        dq.insert(early, away)
        summed = add_up(mine, others, after=dq)
        kept, left = part_ways(dq, after=(summed,))
        kept, left = cross(kept, swap(left, 1))
        dq = unpack_query_grad(kept, swap(concat([x[None] for x in left]), 2), me)
    else:
        summed = add_up(mine, others)
        dq = deal(by_owner(dq[0], groups))
        dq = dq.reshape(heads, tgt // 2, 2, HD).transpose(2, 1, 0, 3).reshape(tgt, width)
    d_memory = lax.all_to_all(summed, "seq", 0, 0, tiled=True)
    return dq, d_memory.reshape(memory.shape)


def solution(mesh):
    return jax.shard_map(
        functools.partial(local, mesh.shape["seq"], mesh.shape["col"]),
        mesh=mesh,
        in_specs=(
            P("col", "seq"),
            P("seq", "col"),
            P("seq", "col"),
            P(None, "col"),
            P(None, "col"),
        ),
        out_specs=(P("seq", "col"), P("col", "seq")),
        check_vma=False,
    )
```

```python
import functools
import math

import jax
import jax.numpy as jnp
from jax import lax
from jax.experimental import pallas as pl
from jax.experimental.pallas import tpu as pltpu
from jax.sharding import PartitionSpec as P

HD = 64
F32 = jnp.float32
BF16 = jnp.bfloat16
VMEM = pl.BlockSpec(memory_space=pltpu.VMEM)
SMEM = pl.BlockSpec(memory_space=pltpu.SMEM)
MIB = 1024 * 1024


def dot(a, b, over_a, over_b):
    return lax.dot_general(
        a, b, (((over_a,), (over_b,)), ((), ())), preferred_element_type=F32
    )


def whole(kernel, out, *args, after=(), scratch=(), limit=16, flops=0):
    n = len(args)
    moved = sum(x.size * x.dtype.itemsize for x in args)
    return pl.pallas_call(
        lambda *refs: kernel(*refs[:n], *refs[n + len(after) :]),
        in_specs=[SMEM if x.dtype == jnp.int32 else VMEM for x in args]
        + [pl.BlockSpec(memory_space=pl.ANY)] * len(after),
        out_specs=[VMEM] * len(out),
        out_shape=out,
        scratch_shapes=scratch,
        compiler_params=pltpu.CompilerParams(vmem_limit_bytes=limit * MIB),
        cost_estimate=pl.CostEstimate(flops=flops, bytes_accessed=moved, transcendentals=0),
    )(*args, *after)


def head_of(x, h):
    return x[:, h * HD : (h + 1) * HD]


def pair_heads(query, out_grad):
    tgt, width = query.shape

    def kernel(q_ref, g_ref, out_ref):
        for h in range(width // HD):
            cols = pl.ds(h * HD, HD)
            out_ref[h] = jnp.concatenate([q_ref[:, cols], g_ref[:, cols]], axis=1)

    out = [jax.ShapeDtypeStruct((width // HD, tgt, 2 * HD), BF16)]
    return whole(kernel, out, query, out_grad)[0]


def pair_targets(query, out_grad, me, spans):
    tgt, width = query.shape
    place = [(i, at) for i, span in enumerate(spans) for at in range(len(span))]
    out = [
        jax.ShapeDtypeStruct((len(span), 2, tgt, 2 * HD), BF16) for span in spans for _ in range(2)
    ]

    def kernel(me_ref, q_ref, g_ref, *rest):
        out_refs, paired = rest[:-1], rest[-1]
        for h in range(width // HD):
            cols = pl.ds(h * HD, HD)
            paired[h] = jnp.concatenate([q_ref[:, cols], g_ref[:, cols]], axis=1)
        for i, at in place:
            for bits in range(4):
                head = (4 * spans[i][at] + bits) ^ me_ref[0]
                out_refs[2 * i + bits // 2][at, bits % 2] = paired[head]

    scratch = [pltpu.VMEM((width // HD, tgt, 2 * HD), BF16)]
    return whole(kernel, out, me, query, out_grad, scratch=scratch)


def cross(kept, came, after=()):
    n = kept.shape[0]

    def kernel(kept_ref, came_ref, first_ref, *second_refs):
        for i, ref in enumerate((kept_ref, came_ref)):
            first_ref[:, i] = ref[:, 0]
            for d, second_ref in enumerate(second_refs):
                second_ref[i] = ref[d, 1]

    out = [jax.ShapeDtypeStruct(kept.shape, kept.dtype)] + [jax.ShapeDtypeStruct(kept.shape[1:], kept.dtype)] * n
    first, *second = whole(kernel, out, kept, came, after=after)
    return first, second


def join(kept, came, after=()):
    def kernel(kept_ref, *refs):
        for d in range(len(came)):
            out_ref = refs[len(came) + d]
            out_ref[0] = kept_ref[d]
            out_ref[1] = refs[d][...]

    out = [jax.ShapeDtypeStruct((2, *kept.shape[1:]), kept.dtype)] * kept.shape[0]
    return whole(kernel, out, kept, *came, after=after)


def part_ways(pieces, after=()):
    def kernel(*refs):
        kept_ref, left_ref = refs[-2:]
        for d, ref in enumerate(refs[:-2]):
            kept_ref[d] = ref[0]
            left_ref[d] = ref[1]

    out = [jax.ShapeDtypeStruct((len(pieces), *pieces[0].shape[1:]), pieces[0].dtype)] * 2
    return whole(kernel, out, *pieces, after=after)


def concat(pieces, after=()):
    rows = [x.shape[0] for x in pieces]

    def kernel(*refs):
        at = 0
        for ref, n in zip(refs[:-1], rows):
            refs[-1][at : at + n] = ref[...]
            at += n

    out = [jax.ShapeDtypeStruct((sum(rows), *pieces[0].shape[1:]), pieces[0].dtype)]
    return whole(kernel, out, *pieces, after=after)[0]


def fetch(arrays, after=()):
    n = len(arrays)

    def kernel(*refs):
        copies = [pltpu.make_async_copy(refs[i], refs[i - n - 1], refs[-1].at[i]) for i in range(n)]
        for copy in copies:
            copy.start()
        for copy in copies:
            copy.wait()

    anywhere = pl.BlockSpec(memory_space=pl.ANY)
    return pl.pallas_call(
        kernel,
        in_specs=[anywhere] * (n + len(after)),
        out_specs=[VMEM] * n,
        out_shape=[pltpu.VMEM(x.shape, x.dtype) for x in arrays],
        scratch_shapes=[pltpu.SemaphoreType.DMA((n,))],
        compiler_params=pltpu.CompilerParams(vmem_limit_bytes=12 * MIB),
        cost_estimate=pl.CostEstimate(
            flops=0, bytes_accessed=sum(x.size * x.dtype.itemsize for x in arrays), transcendentals=0
        ),
    )(*[pltpu.with_memory_space_constraint(x, pltpu.MemorySpace.HBM) for x in arrays], *after)


def project(mems, w_key, w_value, after=()):
    blocks, rows, depth = mems[0].shape
    depth *= blocks
    width = w_key.shape[1]
    heads = width // HD
    tile = math.gcd(width, 256)

    def kernel(k_ref, v_ref, *refs):
        out_ref = refs[-1]
        m = [jnp.concatenate([ref[b] for ref in refs[:-1]], axis=0) for b in range(blocks)]
        m = jnp.concatenate(m, axis=1)
        for at in range(0, width, tile):
            key = dot(m, k_ref[:, at : at + tile], 1, 0).astype(BF16)
            value = dot(m, v_ref[:, at : at + tile], 1, 0).astype(BF16)
            for h in range(tile // HD):
                out_ref[at // HD + h] = jnp.concatenate([head_of(key, h), head_of(value, h)], axis=1)

    total = rows * len(mems)
    out = [jax.ShapeDtypeStruct((heads, total, 2 * HD), BF16)]
    return whole(kernel, out, w_key, w_value, *mems, after=after)[0]


def memory_grad(dkv, at, rows, w_key, w_value, blocks, dtype, span=(0, 1), after=()):
    heads = dkv.shape[0]
    depth, width = w_key.shape
    each = depth // blocks
    tile = max(each, math.gcd(depth, 512))
    low, high = (int(depth * x) // tile * tile for x in span)

    def kernel(d_ref, k_ref, v_ref, out_ref):
        d = [d_ref[h, at : at + rows, :] for h in range(heads)]
        dk = jnp.concatenate([x[:, :HD] for x in d], axis=1)
        dv = jnp.concatenate([x[:, HD:] for x in d], axis=1)
        for start in range(low, high, tile):
            here = pl.ds(start, tile)
            part = dot(k_ref[here, :], dk, 1, 1) + dot(v_ref[here, :], dv, 1, 1)
            part = part.T.astype(dtype)
            for b in range(tile // each):
                out_ref[(start - low) // each + b] = part[:, b * each : (b + 1) * each]

    out = [jax.ShapeDtypeStruct(((high - low) // each, rows, each), dtype)]
    flops = 4 * rows * (high - low) * width
    return whole(kernel, out, dkv, w_key, w_value, after=after, flops=flops)[0]


def add_up(mine, others, after=()):
    half = mine.shape[0] // 2

    def kernel(mine_ref, *refs):
        out_ref = refs[-1]
        for i in range(2):
            here = pl.ds(i * half, half)
            total = mine_ref[here]
            for ref in refs[i:-1:2]:
                total = total + ref[...].astype(F32)
            out_ref[here] = total.astype(BF16)

    out = [jax.ShapeDtypeStruct(mine.shape, BF16)]
    return whole(kernel, out, mine, *others, after=after)[0]


def unpack_query_grad(kept, came, me):
    far, _, half, wide = kept.shape
    heads = 4 * far

    def kernel(me_ref, kept_ref, came_ref, out_ref, by_head):
        for d in range(far):
            for bits in range(4):
                ref = came_ref if bits // 2 else kept_ref
                by_head[(4 * d + bits) ^ me_ref[0]] = ref[d, bits % 2]
        for side in range(2):
            rows = [by_head[h][:, side * HD : (side + 1) * HD] for h in range(heads)]
            out_ref[pl.ds(side * half, half), :] = jnp.concatenate(rows, axis=1)

    out = [jax.ShapeDtypeStruct((2 * half, heads * HD), BF16)]
    return whole(kernel, out, me, kept, came, scratch=[pltpu.VMEM((heads, half, wide), BF16)])[0]


def fold_rows(x, combine):
    return combine(x.reshape(x.shape[0] // 8, 8, x.shape[1]), axis=0)


def attention_kernel(tile, chunk, rows, first, last, qg_ref, kv_ref, *refs):
    step = pl.program_id(1)
    begin = (pl.program_id(0) == 0) & (step == 0)
    end = (pl.program_id(0) == pl.num_programs(0) - 1) & (step == pl.num_programs(1) - 1)
    if not first:
        before_ref, *refs = refs
    if last:
        wk_ref, wv_ref, dq_ref, dkv_ref, wk_out, wv_out, sem, *refs = refs
    else:
        dq_ref, dkv_ref, *refs = refs
    s_ref, e_ref, p_ref, acc_ref, kt_ref = refs

    fetches = []
    if last:
        fetches.append(pltpu.make_async_copy(wk_ref, wk_out, sem.at[0]))
        fetches.append(pltpu.make_async_copy(wv_ref, wv_out, sem.at[1]))

    @pl.when(begin)
    def _():
        for fetch in fetches:
            fetch.start()

    src, tgt = kv_ref.shape[0], qg_ref.shape[0]
    factor = 1.0 / math.sqrt(HD)
    slope = factor * math.log2(math.e)

    @pl.when(step == 0)
    def _():
        acc_ref[...] = jnp.zeros_like(acc_ref) if first else before_ref[...]
        kt_ref[...] = kv_ref[...].T[:HD]

    chunks = [pl.ds(at, chunk) for at in range(0, src, chunk)]
    tiles = tgt // tile

    def load(t):
        qg = qg_ref[pl.ds(pl.multiple_of(t * tile, tile), tile), :]
        in_query = lax.broadcasted_iota(jnp.int32, qg.shape, 1) < HD
        zero = jnp.zeros_like(qg)
        return jnp.where(in_query, qg, zero), jnp.where(in_query, zero, qg)

    def advance(t, carry, scores=True, weigh=True, grads=True):
        last_top, inverse, delta = carry
        top = total = inner = dq = None
        if scores:
            q_only, _ = load(t)
        if weigh:
            _, g_last = load(t - 1)
        if grads:
            q, g = load(t - 2)
            both = jnp.concatenate([g, q], axis=0)
        for here in chunks:
            if grads:
                weights = e_ref[here, :] * inverse
                grad = (weights * (p_ref[here, :] - delta)).astype(BF16)
                pair = jnp.concatenate([weights.astype(BF16), grad], axis=1)
                acc_ref[here, :] += dot(pair, both, 1, 0)
                part = dot(kt_ref[:, here], grad, 1, 0)
                dq = part if dq is None else dq + part
            if weigh:
                expo = jnp.exp2((s_ref[here, :] - last_top) * slope)
                p = dot(kv_ref[here, :], g_last, 1, 1)
                e_ref[here, :] = expo
                p_ref[here, :] = p
                sums = fold_rows(expo, jnp.sum), fold_rows(expo * p, jnp.sum)
                total, inner = sums if total is None else (total + sums[0], inner + sums[1])
            if scores:
                s = dot(kv_ref[here, :], q_only, 1, 1)
                s_ref[here, :] = s
                s = fold_rows(s, jnp.max)
                top = s if top is None else jnp.maximum(top, s)
        if grads:
            dq = (dq * factor).T
            half = rows // 2
            for at in range(0, tile, rows):
                to = pl.multiple_of((t - 2) * (tile // 2) + at // 2, half)
                dq_ref[pl.ds(to, half), :] = jnp.concatenate(
                    [dq[at : at + half], dq[at + half : at + rows]], axis=1
                ).astype(BF16)
        if weigh:
            inverse = 1.0 / jnp.sum(total, axis=0, keepdims=True)
            delta = jnp.sum(inner, axis=0, keepdims=True) * inverse
        if scores:
            last_top = jnp.max(top, axis=0, keepdims=True)
        return last_top, inverse, delta

    nothing = jnp.zeros((1, tile), F32)
    carry = advance(0, (nothing,) * 3, weigh=False, grads=False)
    if tiles > 1:
        carry = advance(1, carry, grads=False)
        carry = lax.fori_loop(2, tiles, advance, carry)
    carry = advance(tiles, carry, scores=False, grads=tiles > 1)
    advance(tiles + 1, carry, scores=False, weigh=False)

    @pl.when(step == pl.num_programs(1) - 1)
    def _():
        acc = acc_ref[...]
        if last:
            in_key = lax.broadcasted_iota(jnp.int32, acc.shape, 1) < HD
            acc = jnp.where(in_key, acc * factor, acc)
        dkv_ref[...] = acc.astype(dkv_ref.dtype)

    @pl.when(end)
    def _():
        for fetch in fetches:
            fetch.wait()


def attention(qg, kv, rows, before=None, weights=(), block=2048, tile=256, chunk=512):
    heads, tgt, wide = qg.shape
    src = kv.shape[1]
    first, last = before is None, bool(weights)
    work = heads * tgt * src
    tile = max(math.gcd(tgt, tile), rows)
    block = max(math.gcd(tgt, block), tile)
    weights = [pltpu.with_memory_space_constraint(w, pltpu.MemorySpace.HBM) for w in weights]
    every = pl.BlockSpec((None, src, wide), lambda h, i: (h, 0, 0))
    anywhere = pl.BlockSpec(memory_space=pl.ANY)
    return pl.pallas_call(
        functools.partial(attention_kernel, tile, math.gcd(src, chunk), rows, first, last),
        grid=(heads, tgt // block),
        in_specs=[pl.BlockSpec((None, block, wide), lambda h, i: (h, i, 0)), every]
        + [every] * (not first)
        + [anywhere] * len(weights),
        out_specs=[pl.BlockSpec((None, block // 2, wide), lambda h, i: (h, i, 0)), every]
        + [anywhere] * len(weights),
        out_shape=[
            jax.ShapeDtypeStruct((heads, tgt // 2, wide), BF16),
            jax.ShapeDtypeStruct((heads, src, wide), BF16 if last else F32),
        ]
        + [pltpu.VMEM(w.shape, w.dtype) for w in weights],
        scratch_shapes=[pltpu.SemaphoreType.DMA((2,))] * last
        + [
            pltpu.VMEM((src, tile), F32),
            pltpu.VMEM((src, tile), F32),
            pltpu.VMEM((src, tile), F32),
            pltpu.VMEM((src, wide), F32),
            pltpu.VMEM((HD, src), BF16),
        ],
        compiler_params=pltpu.CompilerParams(vmem_limit_bytes=32 * MIB),
        cost_estimate=pl.CostEstimate(
            flops=5 * 8 * work * HD, bytes_accessed=8 * heads * (tgt + src) * wide, transcendentals=work
        ),
    )(qg, kv, *(() if first else (before,)), *weights)


def local(seq, col, memory, query, out_grad, w_key, w_value):
    tgt, width = query.shape
    heads = width // HD
    groups = math.gcd(heads, seq)
    ranges = seq // groups
    each = heads // groups
    same_range = [[r * groups + g for g in range(groups)] for r in range(ranges)]
    same_heads = [[r * groups + g for r in range(ranges)] for g in range(groups)]
    pairwise = ranges == 1 and each == 1 and groups >= 16 and groups & (groups - 1) == 0
    me = lax.axis_index("seq").astype(jnp.int32) if pairwise else jnp.int32(0)
    me = me.reshape(1)
    far = groups // 4

    def deal(x):
        return lax.all_to_all(x, "seq", 0, 0, tiled=True, axis_index_groups=same_range)

    def swap(x, bits):
        return lax.ppermute(x, "seq", [(i, i ^ bits) for i in range(seq)])

    def gather_far(x, d):
        return swap(x, 4 * d) if d else x

    def by_head(x, many):
        x = x.reshape(many, each, *x.shape[1:]).swapaxes(0, 1)
        return x.reshape(each, many * x.shape[2], x.shape[3])

    def by_owner(x, many):
        x = x.reshape(each, many, x.shape[1] // many, x.shape[2]).swapaxes(0, 1)
        return x.reshape(many * each, *x.shape[2:])

    def shift(x, by):
        return lax.ppermute(x, "col", [(i, (i + by) % col) for i in range(col)])

    rows = memory.shape[0] // seq
    total = rows * col
    own = lax.all_to_all(memory.reshape(seq, rows, -1), "seq", 0, 0, tiled=True)

    if pairwise:
        early = far // 2
        late = [d for d in range(far) if d != early]
        kept, left, kept_late, left_late = pair_targets(query, out_grad, me, [[early], late])
        kept, left = cross(kept, swap(left, 2))
        early_qg, own = lax.optimization_barrier((join(kept, [swap(x, 1) for x in left])[0], own))
        early_qg = gather_far(early_qg, early)
        left_late = concat([left_late], after=(own,))
        left_late = swap(left_late, 2)
        held = fetch([w_key, w_value], after=(own,))
        kept, left = cross(kept_late, left_late, after=held[:1])
        late_qg = join(kept, [swap(x, 1) for x in left])
        rest = [shift(own, by) for by in range(1, col)]
        kv = project([own, *rest], *held, after=(late_qg[0],))
        early_qg, kv = lax.optimization_barrier((early_qg, kv))
        kv = deal(kv)
        late_qg = [gather_far(x, d) for x, d in zip(late_qg, late)]
        qg = [[late_qg[0], early_qg], late_qg[1:]]
    else:
        qg = deal(pair_heads(query, out_grad))
        kv = deal(project([own, *[shift(own, by) for by in range(1, col)]], w_key, w_value))
        qg = [by_head(qg, groups)]
    if ranges > 1:
        kv = lax.all_gather(kv, "seq", axis=0, tiled=True, axis_index_groups=same_heads)
    kv = by_head(kv, seq)

    dq, dkv = [], None
    for i, x in enumerate(qg):
        if pairwise:
            x = concat([piece.reshape(-1, 2 * HD) for piece in x], after=(dkv,) * (i > 0))[None]
        weights = (w_key, w_value) if i == len(qg) - 1 else ()
        part, dkv, *weights = attention(x, kv, tgt, dkv, weights)
        dq.append(part)
        if pairwise and i == 0:
            home, away = dq.pop().reshape(2, 2, 2, tgt // 2, 2 * HD)
            away = gather_far(away, early)
    w_key, w_value = weights
    if pairwise:
        dkv, away = lax.optimization_barrier((dkv, away))
    dkv = by_owner(dkv, seq)
    if ranges > 1:
        dkv = lax.psum_scatter(dkv, "seq", scatter_dimension=0, tiled=True, axis_index_groups=same_heads)
    dkv = deal(dkv)

    others = [
        (by, memory_grad(dkv, by * rows, rows, w_key, w_value, seq, BF16, span))
        for by in range(1, col)
        for span in ((0, 0.5), (0.5, 1))
    ]
    first = [x for _, x in others]
    others = [shift(x, col - by) for by, x in others]
    mine = memory_grad(dkv, 0, rows, w_key, w_value, seq, F32)
    if pairwise:
        dq = concat([x.reshape(-1, 2, 2, tgt // 2, 2 * HD) for x in dq], after=first)
        dq = [home, *[gather_far(x, d) for x, d in zip(dq, late[1:])]]
        dq.insert(early, away)
        summed = add_up(mine, others, after=dq)
        kept, left = part_ways(dq, after=(summed,))
        kept, left = cross(kept, swap(left, 1))
        dq = unpack_query_grad(kept, swap(concat([x[None] for x in left]), 2), me)
    else:
        summed = add_up(mine, others)
        dq = deal(by_owner(dq[0], groups))
        dq = dq.reshape(heads, tgt // 2, 2, HD).transpose(2, 1, 0, 3).reshape(tgt, width)
    d_memory = lax.all_to_all(summed, "seq", 0, 0, tiled=True)
    return dq, d_memory.reshape(memory.shape)


def solution(mesh):
    return jax.shard_map(
        functools.partial(local, mesh.shape["seq"], mesh.shape["col"]),
        mesh=mesh,
        in_specs=(
            P("col", "seq"),
            P("seq", "col"),
            P("seq", "col"),
            P(None, "col"),
            P(None, "col"),
        ),
        out_specs=(P("seq", "col"), P("col", "seq")),
        check_vma=False,
    )
```

```python
import functools
import math

import jax
import jax.numpy as jnp
from jax import lax
from jax.experimental import pallas as pl
from jax.experimental.pallas import tpu as pltpu
from jax.sharding import PartitionSpec as P

HD = 64
F32 = jnp.float32
BF16 = jnp.bfloat16
VMEM = pl.BlockSpec(memory_space=pltpu.VMEM)
SMEM = pl.BlockSpec(memory_space=pltpu.SMEM)
MIB = 1024 * 1024


def dot(a, b, over_a, over_b):
    return lax.dot_general(
        a, b, (((over_a,), (over_b,)), ((), ())), preferred_element_type=F32
    )


def whole(kernel, out, *args, after=(), scratch=(), limit=16, flops=0):
    n = len(args)
    moved = sum(x.size * x.dtype.itemsize for x in args)
    return pl.pallas_call(
        lambda *refs: kernel(*refs[:n], *refs[n + len(after) :]),
        in_specs=[SMEM if x.dtype == jnp.int32 else VMEM for x in args]
        + [pl.BlockSpec(memory_space=pl.ANY)] * len(after),
        out_specs=[VMEM] * len(out),
        out_shape=out,
        scratch_shapes=scratch,
        compiler_params=pltpu.CompilerParams(vmem_limit_bytes=limit * MIB),
        cost_estimate=pl.CostEstimate(flops=flops, bytes_accessed=moved, transcendentals=0),
    )(*args, *after)


def head_of(x, h):
    return x[:, h * HD : (h + 1) * HD]


def pair_heads(query, out_grad):
    tgt, width = query.shape

    def kernel(q_ref, g_ref, out_ref):
        for h in range(width // HD):
            cols = pl.ds(h * HD, HD)
            out_ref[h] = jnp.concatenate([q_ref[:, cols], g_ref[:, cols]], axis=1)

    out = [jax.ShapeDtypeStruct((width // HD, tgt, 2 * HD), BF16)]
    return whole(kernel, out, query, out_grad)[0]


def pair_targets(query, out_grad, me, spans):
    tgt, width = query.shape
    place = [(i, at) for i, span in enumerate(spans) for at in range(len(span))]
    out = [
        jax.ShapeDtypeStruct((len(span), 2, tgt, 2 * HD), BF16) for span in spans for _ in range(2)
    ]

    def kernel(me_ref, q_ref, g_ref, *rest):
        out_refs, paired = rest[:-1], rest[-1]
        for h in range(width // HD):
            cols = pl.ds(h * HD, HD)
            paired[h] = jnp.concatenate([q_ref[:, cols], g_ref[:, cols]], axis=1)
        for i, at in place:
            for bits in range(4):
                head = (4 * spans[i][at] + bits) ^ me_ref[0]
                out_refs[2 * i + bits // 2][at, bits % 2] = paired[head]

    scratch = [pltpu.VMEM((width // HD, tgt, 2 * HD), BF16)]
    return whole(kernel, out, me, query, out_grad, scratch=scratch)


def cross(kept, came, after=()):
    n = kept.shape[0]

    def kernel(kept_ref, came_ref, first_ref, *second_refs):
        for i, ref in enumerate((kept_ref, came_ref)):
            first_ref[:, i] = ref[:, 0]
            for d, second_ref in enumerate(second_refs):
                second_ref[i] = ref[d, 1]

    out = [jax.ShapeDtypeStruct(kept.shape, kept.dtype)] + [jax.ShapeDtypeStruct(kept.shape[1:], kept.dtype)] * n
    first, *second = whole(kernel, out, kept, came, after=after)
    return first, second


def join(kept, came, after=()):
    def kernel(kept_ref, *refs):
        for d in range(len(came)):
            out_ref = refs[len(came) + d]
            out_ref[0] = kept_ref[d]
            out_ref[1] = refs[d][...]

    out = [jax.ShapeDtypeStruct((2, *kept.shape[1:]), kept.dtype)] * kept.shape[0]
    return whole(kernel, out, kept, *came, after=after)


def part_ways(pieces, after=()):
    def kernel(*refs):
        kept_ref, left_ref = refs[-2:]
        for d, ref in enumerate(refs[:-2]):
            kept_ref[d] = ref[0]
            left_ref[d] = ref[1]

    out = [jax.ShapeDtypeStruct((len(pieces), *pieces[0].shape[1:]), pieces[0].dtype)] * 2
    return whole(kernel, out, *pieces, after=after)


def concat(pieces, after=()):
    rows = [x.shape[0] for x in pieces]

    def kernel(*refs):
        at = 0
        for ref, n in zip(refs[:-1], rows):
            refs[-1][at : at + n] = ref[...]
            at += n

    out = [jax.ShapeDtypeStruct((sum(rows), *pieces[0].shape[1:]), pieces[0].dtype)]
    return whole(kernel, out, *pieces, after=after)[0]


def fetch(arrays, after=()):
    n = len(arrays)

    def kernel(*refs):
        copies = [pltpu.make_async_copy(refs[i], refs[i - n - 1], refs[-1].at[i]) for i in range(n)]
        for copy in copies:
            copy.start()
        for copy in copies:
            copy.wait()

    anywhere = pl.BlockSpec(memory_space=pl.ANY)
    return pl.pallas_call(
        kernel,
        in_specs=[anywhere] * (n + len(after)),
        out_specs=[VMEM] * n,
        out_shape=[pltpu.VMEM(x.shape, x.dtype) for x in arrays],
        scratch_shapes=[pltpu.SemaphoreType.DMA((n,))],
        compiler_params=pltpu.CompilerParams(vmem_limit_bytes=12 * MIB),
        cost_estimate=pl.CostEstimate(
            flops=0, bytes_accessed=sum(x.size * x.dtype.itemsize for x in arrays), transcendentals=0
        ),
    )(*[pltpu.with_memory_space_constraint(x, pltpu.MemorySpace.HBM) for x in arrays], *after)


def project(mems, w_key, w_value, after=()):
    blocks, rows, depth = mems[0].shape
    depth *= blocks
    width = w_key.shape[1]
    heads = width // HD
    tile = math.gcd(width, 256)

    def kernel(k_ref, v_ref, *refs):
        out_ref = refs[-1]
        m = [jnp.concatenate([ref[b] for ref in refs[:-1]], axis=0) for b in range(blocks)]
        m = jnp.concatenate(m, axis=1)
        for at in range(0, width, tile):
            key = dot(m, k_ref[:, at : at + tile], 1, 0).astype(BF16)
            value = dot(m, v_ref[:, at : at + tile], 1, 0).astype(BF16)
            for h in range(tile // HD):
                out_ref[at // HD + h] = jnp.concatenate([head_of(key, h), head_of(value, h)], axis=1)

    total = rows * len(mems)
    out = [jax.ShapeDtypeStruct((heads, total, 2 * HD), BF16)]
    return whole(kernel, out, w_key, w_value, *mems, after=after)[0]


def project_half(own, rest, w_key, w_value, low, before=(), after=()):
    blocks, rows, each = own.shape
    blocks //= 2
    width = w_key.shape[1]
    heads = width // HD
    tile = math.gcd(width, 256)
    total = rows * (1 + len(rest))
    here = pl.ds(low * each, blocks * each)

    def kernel(k_ref, v_ref, own_ref, *refs):
        rest_refs, refs = refs[: len(rest)], refs[len(rest) :]
        m = [
            jnp.concatenate([own_ref[low + b], *[ref[b] for ref in rest_refs]], axis=0) for b in range(blocks)
        ]
        m = jnp.concatenate(m, axis=1)
        for at in range(0, width, tile):
            cols = slice(at, at + tile)
            key = dot(m, k_ref[here, cols], 1, 0)
            value = dot(m, v_ref[here, cols], 1, 0)
            if not before:
                refs[0][:, cols] = key
                refs[1][:, cols] = value
                continue
            key = (key + refs[0][:, cols]).astype(BF16)
            value = (value + refs[1][:, cols]).astype(BF16)
            for h in range(tile // HD):
                refs[2][at // HD + h] = jnp.concatenate([head_of(key, h), head_of(value, h)], axis=1)

    out = [jax.ShapeDtypeStruct((total, width), F32)] * 2
    if before:
        out = [jax.ShapeDtypeStruct((heads, total, 2 * HD), BF16)]
    return whole(kernel, out, w_key, w_value, own, *rest, *before, after=after)


def memory_grad(dkv, at, rows, w_key, w_value, blocks, dtype, span=(0, 1), after=()):
    heads = dkv.shape[0]
    depth, width = w_key.shape
    each = depth // blocks
    tile = max(each, math.gcd(depth, 512))
    low, high = (int(depth * x) // tile * tile for x in span)

    def kernel(d_ref, k_ref, v_ref, out_ref):
        d = [d_ref[h, at : at + rows, :] for h in range(heads)]
        dk = jnp.concatenate([x[:, :HD] for x in d], axis=1)
        dv = jnp.concatenate([x[:, HD:] for x in d], axis=1)
        for start in range(low, high, tile):
            here = pl.ds(start, tile)
            part = dot(k_ref[here, :], dk, 1, 1) + dot(v_ref[here, :], dv, 1, 1)
            part = part.T.astype(dtype)
            for b in range(tile // each):
                out_ref[(start - low) // each + b] = part[:, b * each : (b + 1) * each]

    out = [jax.ShapeDtypeStruct(((high - low) // each, rows, each), dtype)]
    flops = 4 * rows * (high - low) * width
    return whole(kernel, out, dkv, w_key, w_value, after=after, flops=flops)[0]


def add_up(mine, others, after=()):
    half = mine.shape[0] // 2

    def kernel(mine_ref, *refs):
        out_ref = refs[-1]
        for i in range(2):
            here = pl.ds(i * half, half)
            total = mine_ref[here]
            for ref in refs[i:-1:2]:
                total = total + ref[...].astype(F32)
            out_ref[here] = total.astype(BF16)

    out = [jax.ShapeDtypeStruct(mine.shape, BF16)]
    return whole(kernel, out, mine, *others, after=after)[0]


def unpack_query_grad(kept, came, me):
    far, _, half, wide = kept.shape
    heads = 4 * far

    def kernel(me_ref, kept_ref, came_ref, out_ref, by_head):
        for d in range(far):
            for bits in range(4):
                ref = came_ref if bits // 2 else kept_ref
                by_head[(4 * d + bits) ^ me_ref[0]] = ref[d, bits % 2]
        for side in range(2):
            rows = [by_head[h][:, side * HD : (side + 1) * HD] for h in range(heads)]
            out_ref[pl.ds(side * half, half), :] = jnp.concatenate(rows, axis=1)

    out = [jax.ShapeDtypeStruct((2 * half, heads * HD), BF16)]
    return whole(kernel, out, me, kept, came, scratch=[pltpu.VMEM((heads, half, wide), BF16)])[0]


def fold_rows(x, combine):
    return combine(x.reshape(x.shape[0] // 8, 8, x.shape[1]), axis=0)


def attention_kernel(tile, chunk, rows, first, last, qg_ref, kv_ref, *refs):
    step = pl.program_id(1)
    begin = (pl.program_id(0) == 0) & (step == 0)
    end = (pl.program_id(0) == pl.num_programs(0) - 1) & (step == pl.num_programs(1) - 1)
    if not first:
        before_ref, *refs = refs
    if last:
        wk_ref, wv_ref, dq_ref, dkv_ref, wk_out, wv_out, sem, *refs = refs
    else:
        dq_ref, dkv_ref, *refs = refs
    s_ref, e_ref, p_ref, acc_ref, kt_ref = refs

    fetches = []
    if last:
        fetches.append(pltpu.make_async_copy(wk_ref, wk_out, sem.at[0]))
        fetches.append(pltpu.make_async_copy(wv_ref, wv_out, sem.at[1]))

    @pl.when(begin)
    def _():
        for fetch in fetches:
            fetch.start()

    src, tgt = kv_ref.shape[0], qg_ref.shape[0]
    factor = 1.0 / math.sqrt(HD)
    slope = factor * math.log2(math.e)

    @pl.when(step == 0)
    def _():
        acc_ref[...] = jnp.zeros_like(acc_ref) if first else before_ref[...]
        kt_ref[...] = kv_ref[...].T[:HD]

    chunks = [pl.ds(at, chunk) for at in range(0, src, chunk)]
    tiles = tgt // tile

    def load(t):
        qg = qg_ref[pl.ds(pl.multiple_of(t * tile, tile), tile), :]
        in_query = lax.broadcasted_iota(jnp.int32, qg.shape, 1) < HD
        zero = jnp.zeros_like(qg)
        return jnp.where(in_query, qg, zero), jnp.where(in_query, zero, qg)

    def advance(t, carry, scores=True, weigh=True, grads=True):
        last_top, inverse, delta = carry
        top = total = inner = dq = None
        if scores:
            q_only, _ = load(t)
        if weigh:
            _, g_last = load(t - 1)
        if grads:
            q, g = load(t - 2)
            both = jnp.concatenate([g, q], axis=0)
        for here in chunks:
            if grads:
                weights = e_ref[here, :] * inverse
                grad = (weights * (p_ref[here, :] - delta)).astype(BF16)
                pair = jnp.concatenate([weights.astype(BF16), grad], axis=1)
                acc_ref[here, :] += dot(pair, both, 1, 0)
                part = dot(kt_ref[:, here], grad, 1, 0)
                dq = part if dq is None else dq + part
            if weigh:
                expo = jnp.exp2((s_ref[here, :] - last_top) * slope)
                p = dot(kv_ref[here, :], g_last, 1, 1)
                e_ref[here, :] = expo
                p_ref[here, :] = p
                sums = fold_rows(expo, jnp.sum), fold_rows(expo * p, jnp.sum)
                total, inner = sums if total is None else (total + sums[0], inner + sums[1])
            if scores:
                s = dot(kv_ref[here, :], q_only, 1, 1)
                s_ref[here, :] = s
                s = fold_rows(s, jnp.max)
                top = s if top is None else jnp.maximum(top, s)
        if grads:
            dq = (dq * factor).T
            half = rows // 2
            for at in range(0, tile, rows):
                to = pl.multiple_of((t - 2) * (tile // 2) + at // 2, half)
                dq_ref[pl.ds(to, half), :] = jnp.concatenate(
                    [dq[at : at + half], dq[at + half : at + rows]], axis=1
                ).astype(BF16)
        if weigh:
            inverse = 1.0 / jnp.sum(total, axis=0, keepdims=True)
            delta = jnp.sum(inner, axis=0, keepdims=True) * inverse
        if scores:
            last_top = jnp.max(top, axis=0, keepdims=True)
        return last_top, inverse, delta

    nothing = jnp.zeros((1, tile), F32)
    carry = advance(0, (nothing,) * 3, weigh=False, grads=False)
    if tiles > 1:
        carry = advance(1, carry, grads=False)
        carry = lax.fori_loop(2, tiles, advance, carry)
    carry = advance(tiles, carry, scores=False, grads=tiles > 1)
    advance(tiles + 1, carry, scores=False, weigh=False)

    @pl.when(step == pl.num_programs(1) - 1)
    def _():
        acc = acc_ref[...]
        if last:
            in_key = lax.broadcasted_iota(jnp.int32, acc.shape, 1) < HD
            acc = jnp.where(in_key, acc * factor, acc)
        dkv_ref[...] = acc.astype(dkv_ref.dtype)

    @pl.when(end)
    def _():
        for fetch in fetches:
            fetch.wait()


def attention(qg, kv, rows, before=None, weights=(), block=2048, tile=256, chunk=512):
    heads, tgt, wide = qg.shape
    src = kv.shape[1]
    first, last = before is None, bool(weights)
    work = heads * tgt * src
    tile = max(math.gcd(tgt, tile), rows)
    block = max(math.gcd(tgt, block), tile)
    weights = [pltpu.with_memory_space_constraint(w, pltpu.MemorySpace.HBM) for w in weights]
    every = pl.BlockSpec((None, src, wide), lambda h, i: (h, 0, 0))
    anywhere = pl.BlockSpec(memory_space=pl.ANY)
    return pl.pallas_call(
        functools.partial(attention_kernel, tile, math.gcd(src, chunk), rows, first, last),
        grid=(heads, tgt // block),
        in_specs=[pl.BlockSpec((None, block, wide), lambda h, i: (h, i, 0)), every]
        + [every] * (not first)
        + [anywhere] * len(weights),
        out_specs=[pl.BlockSpec((None, block // 2, wide), lambda h, i: (h, i, 0)), every]
        + [anywhere] * len(weights),
        out_shape=[
            jax.ShapeDtypeStruct((heads, tgt // 2, wide), BF16),
            jax.ShapeDtypeStruct((heads, src, wide), BF16 if last else F32),
        ]
        + [pltpu.VMEM(w.shape, w.dtype) for w in weights],
        scratch_shapes=[pltpu.SemaphoreType.DMA((2,))] * last
        + [
            pltpu.VMEM((src, tile), F32),
            pltpu.VMEM((src, tile), F32),
            pltpu.VMEM((src, tile), F32),
            pltpu.VMEM((src, wide), F32),
            pltpu.VMEM((HD, src), BF16),
        ],
        compiler_params=pltpu.CompilerParams(vmem_limit_bytes=32 * MIB),
        cost_estimate=pl.CostEstimate(
            flops=5 * 8 * work * HD, bytes_accessed=8 * heads * (tgt + src) * wide, transcendentals=work
        ),
    )(qg, kv, *(() if first else (before,)), *weights)


def local(seq, col, memory, query, out_grad, w_key, w_value):
    tgt, width = query.shape
    heads = width // HD
    groups = math.gcd(heads, seq)
    ranges = seq // groups
    each = heads // groups
    same_range = [[r * groups + g for g in range(groups)] for r in range(ranges)]
    same_heads = [[r * groups + g for r in range(ranges)] for g in range(groups)]
    pairwise = ranges == 1 and each == 1 and groups >= 16 and groups & (groups - 1) == 0
    me = lax.axis_index("seq").astype(jnp.int32) if pairwise else jnp.int32(0)
    me = me.reshape(1)
    far = groups // 4

    def deal(x):
        return lax.all_to_all(x, "seq", 0, 0, tiled=True, axis_index_groups=same_range)

    def swap(x, bits):
        return lax.ppermute(x, "seq", [(i, i ^ bits) for i in range(seq)])

    def gather_far(x, d):
        return swap(x, 4 * d) if d else x

    def by_head(x, many):
        x = x.reshape(many, each, *x.shape[1:]).swapaxes(0, 1)
        return x.reshape(each, many * x.shape[2], x.shape[3])

    def by_owner(x, many):
        x = x.reshape(each, many, x.shape[1] // many, x.shape[2]).swapaxes(0, 1)
        return x.reshape(many * each, *x.shape[2:])

    def shift(x, by):
        return lax.ppermute(x, "col", [(i, (i + by) % col) for i in range(col)])

    rows = memory.shape[0] // seq
    total = rows * col
    own = lax.all_to_all(memory.reshape(seq, rows, -1), "seq", 0, 0, tiled=True)

    if pairwise:
        early = far // 2
        late = [d for d in range(far) if d != early]
        kept, left, kept_late, left_late = pair_targets(query, out_grad, me, [[early], late])
        kept, left = cross(kept, swap(left, 2))
        early_qg, own = lax.optimization_barrier((join(kept, [swap(x, 1) for x in left])[0], own))
        early_qg = gather_far(early_qg, early)
        left_late = concat([left_late], after=(own,))
        left_late = swap(left_late, 2)
        held = fetch([w_key, w_value], after=(own,))
        kept, left = cross(kept_late, left_late, after=held[:1])
        late_qg = join(kept, [swap(x, 1) for x in left])
        half = seq // 2
        rest = [[shift(x, by) for by in range(1, col)] for x in (own[:half], own[half:])]
        sums = project_half(own, rest[0], *held, 0)
        kv = project_half(own, rest[1], *held, half, sums, after=(late_qg[0],))[0]
        early_qg, kv = lax.optimization_barrier((early_qg, kv))
        kv = deal(kv)
        late_qg = [gather_far(x, d) for x, d in zip(late_qg, late)]
        qg = [[late_qg[0], early_qg], late_qg[1:]]
    else:
        qg = deal(pair_heads(query, out_grad))
        kv = deal(project([own, *[shift(own, by) for by in range(1, col)]], w_key, w_value))
        qg = [by_head(qg, groups)]
    if ranges > 1:
        kv = lax.all_gather(kv, "seq", axis=0, tiled=True, axis_index_groups=same_heads)
    kv = by_head(kv, seq)

    dq, dkv = [], None
    for i, x in enumerate(qg):
        if pairwise:
            x = concat([piece.reshape(-1, 2 * HD) for piece in x], after=(dkv,) * (i > 0))[None]
        weights = (w_key, w_value) if i == len(qg) - 1 else ()
        part, dkv, *weights = attention(x, kv, tgt, dkv, weights)
        dq.append(part)
        if pairwise and i == 0:
            home, away = dq.pop().reshape(2, 2, 2, tgt // 2, 2 * HD)
            away = gather_far(away, early)
    w_key, w_value = weights
    if pairwise:
        dkv, away = lax.optimization_barrier((dkv, away))
    dkv = by_owner(dkv, seq)
    if ranges > 1:
        dkv = lax.psum_scatter(dkv, "seq", scatter_dimension=0, tiled=True, axis_index_groups=same_heads)
    dkv = deal(dkv)

    others = [
        (by, memory_grad(dkv, by * rows, rows, w_key, w_value, seq, BF16, span))
        for by in range(1, col)
        for span in ((0, 0.5), (0.5, 1))
    ]
    first = [x for _, x in others]
    others = [shift(x, col - by) for by, x in others]
    mine = memory_grad(dkv, 0, rows, w_key, w_value, seq, F32)
    if pairwise:
        dq = concat([x.reshape(-1, 2, 2, tgt // 2, 2 * HD) for x in dq], after=first)
        dq = [home, *[gather_far(x, d) for x, d in zip(dq, late[1:])]]
        dq.insert(early, away)
        summed = add_up(mine, others, after=dq)
        kept, left = part_ways(dq, after=(summed,))
        kept, left = cross(kept, swap(left, 1))
        dq = unpack_query_grad(kept, swap(concat([x[None] for x in left]), 2), me)
    else:
        summed = add_up(mine, others)
        dq = deal(by_owner(dq[0], groups))
        dq = dq.reshape(heads, tgt // 2, 2, HD).transpose(2, 1, 0, 3).reshape(tgt, width)
    d_memory = lax.all_to_all(summed, "seq", 0, 0, tiled=True)
    return dq, d_memory.reshape(memory.shape)


def solution(mesh):
    return jax.shard_map(
        functools.partial(local, mesh.shape["seq"], mesh.shape["col"]),
        mesh=mesh,
        in_specs=(
            P("col", "seq"),
            P("seq", "col"),
            P("seq", "col"),
            P(None, "col"),
            P(None, "col"),
        ),
        out_specs=(P("seq", "col"), P("col", "seq")),
        check_vma=False,
    )
```

```python
import functools
import math

import jax
import jax.numpy as jnp
from jax import lax
from jax.experimental import pallas as pl
from jax.experimental.pallas import tpu as pltpu
from jax.sharding import PartitionSpec as P

HD = 64
F32 = jnp.float32
BF16 = jnp.bfloat16
VMEM = pl.BlockSpec(memory_space=pltpu.VMEM)
SMEM = pl.BlockSpec(memory_space=pltpu.SMEM)
MIB = 1024 * 1024


def dot(a, b, over_a, over_b):
    return lax.dot_general(
        a, b, (((over_a,), (over_b,)), ((), ())), preferred_element_type=F32
    )


def whole(kernel, out, *args, after=(), scratch=(), limit=16, flops=0):
    n = len(args)
    moved = sum(x.size * x.dtype.itemsize for x in args)
    return pl.pallas_call(
        lambda *refs: kernel(*refs[:n], *refs[n + len(after) :]),
        in_specs=[SMEM if x.dtype == jnp.int32 else VMEM for x in args]
        + [pl.BlockSpec(memory_space=pl.ANY)] * len(after),
        out_specs=[VMEM] * len(out),
        out_shape=out,
        scratch_shapes=scratch,
        compiler_params=pltpu.CompilerParams(vmem_limit_bytes=limit * MIB),
        cost_estimate=pl.CostEstimate(flops=flops, bytes_accessed=moved, transcendentals=0),
    )(*args, *after)


def head_of(x, h):
    return x[:, h * HD : (h + 1) * HD]


def pair_heads(query, out_grad):
    tgt, width = query.shape

    def kernel(q_ref, g_ref, out_ref):
        for h in range(width // HD):
            cols = pl.ds(h * HD, HD)
            out_ref[h] = jnp.concatenate([q_ref[:, cols], g_ref[:, cols]], axis=1)

    out = [jax.ShapeDtypeStruct((width // HD, tgt, 2 * HD), BF16)]
    return whole(kernel, out, query, out_grad)[0]


def pair_targets(query, out_grad, me, spans):
    tgt, width = query.shape
    place = [(i, at) for i, span in enumerate(spans) for at in range(len(span))]
    out = [
        jax.ShapeDtypeStruct((len(span), 2, tgt, 2 * HD), BF16) for span in spans for _ in range(2)
    ]

    def kernel(me_ref, q_ref, g_ref, *rest):
        out_refs, paired = rest[:-1], rest[-1]
        for h in range(width // HD):
            cols = pl.ds(h * HD, HD)
            paired[h] = jnp.concatenate([q_ref[:, cols], g_ref[:, cols]], axis=1)
        for i, at in place:
            for bits in range(4):
                head = (4 * spans[i][at] + bits) ^ me_ref[0]
                out_refs[2 * i + bits // 2][at, bits % 2] = paired[head]

    scratch = [pltpu.VMEM((width // HD, tgt, 2 * HD), BF16)]
    return whole(kernel, out, me, query, out_grad, scratch=scratch)


def cross(kept, came, after=()):
    n = kept.shape[0]

    def kernel(kept_ref, came_ref, first_ref, *second_refs):
        for i, ref in enumerate((kept_ref, came_ref)):
            first_ref[:, i] = ref[:, 0]
            for d, second_ref in enumerate(second_refs):
                second_ref[i] = ref[d, 1]

    out = [jax.ShapeDtypeStruct(kept.shape, kept.dtype)] + [jax.ShapeDtypeStruct(kept.shape[1:], kept.dtype)] * n
    first, *second = whole(kernel, out, kept, came, after=after)
    return first, second


def join(kept, came, after=()):
    def kernel(kept_ref, *refs):
        for d in range(len(came)):
            out_ref = refs[len(came) + d]
            out_ref[0] = kept_ref[d]
            out_ref[1] = refs[d][...]

    out = [jax.ShapeDtypeStruct((2, *kept.shape[1:]), kept.dtype)] * kept.shape[0]
    return whole(kernel, out, kept, *came, after=after)


def part_ways(pieces, after=()):
    def kernel(*refs):
        kept_ref, left_ref = refs[-2:]
        for d, ref in enumerate(refs[:-2]):
            kept_ref[d] = ref[0]
            left_ref[d] = ref[1]

    out = [jax.ShapeDtypeStruct((len(pieces), *pieces[0].shape[1:]), pieces[0].dtype)] * 2
    return whole(kernel, out, *pieces, after=after)


def concat(pieces, after=()):
    rows = [x.shape[0] for x in pieces]

    def kernel(*refs):
        at = 0
        for ref, n in zip(refs[:-1], rows):
            refs[-1][at : at + n] = ref[...]
            at += n

    out = [jax.ShapeDtypeStruct((sum(rows), *pieces[0].shape[1:]), pieces[0].dtype)]
    return whole(kernel, out, *pieces, after=after)[0]


def fetch(arrays, after=()):
    n = len(arrays)

    def kernel(*refs):
        copies = [pltpu.make_async_copy(refs[i], refs[i - n - 1], refs[-1].at[i]) for i in range(n)]
        for copy in copies:
            copy.start()
        for copy in copies:
            copy.wait()

    anywhere = pl.BlockSpec(memory_space=pl.ANY)
    return pl.pallas_call(
        kernel,
        in_specs=[anywhere] * (n + len(after)),
        out_specs=[VMEM] * n,
        out_shape=[pltpu.VMEM(x.shape, x.dtype) for x in arrays],
        scratch_shapes=[pltpu.SemaphoreType.DMA((n,))],
        compiler_params=pltpu.CompilerParams(vmem_limit_bytes=12 * MIB),
        cost_estimate=pl.CostEstimate(
            flops=0, bytes_accessed=sum(x.size * x.dtype.itemsize for x in arrays), transcendentals=0
        ),
    )(*[pltpu.with_memory_space_constraint(x, pltpu.MemorySpace.HBM) for x in arrays], *after)


def project(mems, w_key, w_value, after=()):
    blocks, rows, depth = mems[0].shape
    depth *= blocks
    width = w_key.shape[1]
    heads = width // HD
    tile = math.gcd(width, 256)

    def kernel(k_ref, v_ref, *refs):
        out_ref = refs[-1]
        m = [jnp.concatenate([ref[b] for ref in refs[:-1]], axis=0) for b in range(blocks)]
        m = jnp.concatenate(m, axis=1)
        for at in range(0, width, tile):
            key = dot(m, k_ref[:, at : at + tile], 1, 0).astype(BF16)
            value = dot(m, v_ref[:, at : at + tile], 1, 0).astype(BF16)
            for h in range(tile // HD):
                out_ref[at // HD + h] = jnp.concatenate([head_of(key, h), head_of(value, h)], axis=1)

    total = rows * len(mems)
    out = [jax.ShapeDtypeStruct((heads, total, 2 * HD), BF16)]
    return whole(kernel, out, w_key, w_value, *mems, after=after)[0]


def project_half(own, rest, w_key, w_value, low, before=(), after=()):
    blocks, rows, each = own.shape
    blocks //= 2
    width = w_key.shape[1]
    heads = width // HD
    tile = math.gcd(width, 256)
    total = rows * (1 + len(rest))
    here = pl.ds(low * each, blocks * each)

    def kernel(k_ref, v_ref, own_ref, *refs):
        rest_refs, refs = refs[: len(rest)], refs[len(rest) :]
        m = [
            jnp.concatenate([own_ref[low + b], *[ref[b] for ref in rest_refs]], axis=0) for b in range(blocks)
        ]
        m = jnp.concatenate(m, axis=1)
        for at in range(0, width, tile):
            cols = slice(at, at + tile)
            key = dot(m, k_ref[here, cols], 1, 0)
            value = dot(m, v_ref[here, cols], 1, 0)
            if not before:
                refs[0][:, cols] = key
                refs[1][:, cols] = value
                continue
            key = (key + refs[0][:, cols]).astype(BF16)
            value = (value + refs[1][:, cols]).astype(BF16)
            for h in range(tile // HD):
                refs[2][at // HD + h] = jnp.concatenate([head_of(key, h), head_of(value, h)], axis=1)

    out = [jax.ShapeDtypeStruct((total, width), F32)] * 2
    if before:
        out = [jax.ShapeDtypeStruct((heads, total, 2 * HD), BF16)]
    return whole(kernel, out, w_key, w_value, own, *rest, *before, after=after)


def memory_grad(dkv, at, rows, w_key, w_value, blocks, dtype, span=(0, 1), after=()):
    heads = dkv.shape[0]
    depth, width = w_key.shape
    each = depth // blocks
    tile = max(each, math.gcd(depth, 512))
    low, high = (int(depth * x) // tile * tile for x in span)

    def kernel(d_ref, k_ref, v_ref, out_ref):
        d = [d_ref[h, at : at + rows, :] for h in range(heads)]
        dk = jnp.concatenate([x[:, :HD] for x in d], axis=1)
        dv = jnp.concatenate([x[:, HD:] for x in d], axis=1)
        for start in range(low, high, tile):
            here = pl.ds(start, tile)
            part = dot(k_ref[here, :], dk, 1, 1) + dot(v_ref[here, :], dv, 1, 1)
            part = part.T.astype(dtype)
            for b in range(tile // each):
                out_ref[(start - low) // each + b] = part[:, b * each : (b + 1) * each]

    out = [jax.ShapeDtypeStruct(((high - low) // each, rows, each), dtype)]
    flops = 4 * rows * (high - low) * width
    return whole(kernel, out, dkv, w_key, w_value, after=after, flops=flops)[0]


def add_up(mine, others, after=()):
    half = mine.shape[0] // 2

    def kernel(mine_ref, *refs):
        out_ref = refs[-1]
        for i in range(2):
            here = pl.ds(i * half, half)
            total = mine_ref[here]
            for ref in refs[i:-1:2]:
                total = total + ref[...].astype(F32)
            out_ref[here] = total.astype(BF16)

    out = [jax.ShapeDtypeStruct(mine.shape, BF16)]
    return whole(kernel, out, mine, *others, after=after)[0]


def unpack_query_grad(kept, came, me):
    far, _, half, wide = kept.shape
    heads = 4 * far

    def kernel(me_ref, kept_ref, came_ref, out_ref, by_head):
        for d in range(far):
            for bits in range(4):
                ref = came_ref if bits // 2 else kept_ref
                by_head[(4 * d + bits) ^ me_ref[0]] = ref[d, bits % 2]
        for side in range(2):
            rows = [by_head[h][:, side * HD : (side + 1) * HD] for h in range(heads)]
            out_ref[pl.ds(side * half, half), :] = jnp.concatenate(rows, axis=1)

    out = [jax.ShapeDtypeStruct((2 * half, heads * HD), BF16)]
    return whole(kernel, out, me, kept, came, scratch=[pltpu.VMEM((heads, half, wide), BF16)])[0]


def fold_rows(x, combine):
    return combine(x.reshape(x.shape[0] // 8, 8, x.shape[1]), axis=0)


def attention_kernel(tile, chunk, rows, first, last, qg_ref, kv_ref, *refs):
    step = pl.program_id(1)
    begin = (pl.program_id(0) == 0) & (step == 0)
    end = (pl.program_id(0) == pl.num_programs(0) - 1) & (step == pl.num_programs(1) - 1)
    if not first:
        before_ref, *refs = refs
    if last:
        wk_ref, wv_ref, dq_ref, dkv_ref, wk_out, wv_out, sem, *refs = refs
    else:
        dq_ref, dkv_ref, *refs = refs
    s_ref, e_ref, p_ref, acc_ref, kt_ref = refs

    fetches = []
    if last:
        fetches.append(pltpu.make_async_copy(wk_ref, wk_out, sem.at[0]))
        fetches.append(pltpu.make_async_copy(wv_ref, wv_out, sem.at[1]))

    @pl.when(begin)
    def _():
        for fetch in fetches:
            fetch.start()

    src, tgt = kv_ref.shape[0], qg_ref.shape[0]
    factor = 1.0 / math.sqrt(HD)
    slope = factor * math.log2(math.e)

    @pl.when(step == 0)
    def _():
        acc_ref[...] = jnp.zeros_like(acc_ref) if first else before_ref[...]
        kt_ref[...] = kv_ref[...].T[:HD]

    chunks = [pl.ds(at, chunk) for at in range(0, src, chunk)]
    tiles = tgt // tile

    def load(t):
        qg = qg_ref[pl.ds(pl.multiple_of(t * tile, tile), tile), :]
        in_query = lax.broadcasted_iota(jnp.int32, qg.shape, 1) < HD
        zero = jnp.zeros_like(qg)
        return jnp.where(in_query, qg, zero), jnp.where(in_query, zero, qg)

    def advance(t, carry, scores=True, weigh=True, grads=True):
        last_top, inverse, delta = carry
        top = total = inner = dq = None
        if scores:
            q_only, _ = load(t)
        if weigh:
            _, g_last = load(t - 1)
        if grads:
            q, g = load(t - 2)
            both = jnp.concatenate([g, q], axis=0)
        for here in chunks:
            if grads:
                weights = e_ref[here, :] * inverse
                grad = (weights * (p_ref[here, :] - delta)).astype(BF16)
                pair = jnp.concatenate([weights.astype(BF16), grad], axis=1)
                acc_ref[here, :] += dot(pair, both, 1, 0)
                part = dot(kt_ref[:, here], grad, 1, 0)
                dq = part if dq is None else dq + part
            if weigh:
                expo = jnp.exp2((s_ref[here, :] - last_top) * slope)
                p = dot(kv_ref[here, :], g_last, 1, 1)
                e_ref[here, :] = expo
                p_ref[here, :] = p
                sums = fold_rows(expo, jnp.sum), fold_rows(expo * p, jnp.sum)
                total, inner = sums if total is None else (total + sums[0], inner + sums[1])
            if scores:
                s = dot(kv_ref[here, :], q_only, 1, 1)
                s_ref[here, :] = s
                s = fold_rows(s, jnp.max)
                top = s if top is None else jnp.maximum(top, s)
        if grads:
            dq = (dq * factor).T
            half = rows // 2
            for at in range(0, tile, rows):
                to = pl.multiple_of((t - 2) * (tile // 2) + at // 2, half)
                dq_ref[pl.ds(to, half), :] = jnp.concatenate(
                    [dq[at : at + half], dq[at + half : at + rows]], axis=1
                ).astype(BF16)
        if weigh:
            inverse = 1.0 / jnp.sum(total, axis=0, keepdims=True)
            delta = jnp.sum(inner, axis=0, keepdims=True) * inverse
        if scores:
            last_top = jnp.max(top, axis=0, keepdims=True)
        return last_top, inverse, delta

    nothing = jnp.zeros((1, tile), F32)
    carry = advance(0, (nothing,) * 3, weigh=False, grads=False)
    if tiles > 1:
        carry = advance(1, carry, grads=False)
        carry = lax.fori_loop(2, tiles, advance, carry)
    carry = advance(tiles, carry, scores=False, grads=tiles > 1)
    advance(tiles + 1, carry, scores=False, weigh=False)

    @pl.when(step == pl.num_programs(1) - 1)
    def _():
        acc = acc_ref[...]
        if last:
            in_key = lax.broadcasted_iota(jnp.int32, acc.shape, 1) < HD
            acc = jnp.where(in_key, acc * factor, acc)
        dkv_ref[...] = acc.astype(dkv_ref.dtype)

    @pl.when(end)
    def _():
        for fetch in fetches:
            fetch.wait()


def attention(qg, kv, rows, before=None, weights=(), block=2048, tile=512, chunk=512):
    heads, tgt, wide = qg.shape
    src = kv.shape[1]
    first, last = before is None, bool(weights)
    work = heads * tgt * src
    tile = max(math.gcd(tgt, tile), rows)
    block = max(math.gcd(tgt, block), tile)
    weights = [pltpu.with_memory_space_constraint(w, pltpu.MemorySpace.HBM) for w in weights]
    every = pl.BlockSpec((None, src, wide), lambda h, i: (h, 0, 0))
    anywhere = pl.BlockSpec(memory_space=pl.ANY)
    return pl.pallas_call(
        functools.partial(attention_kernel, tile, math.gcd(src, chunk), rows, first, last),
        grid=(heads, tgt // block),
        in_specs=[pl.BlockSpec((None, block, wide), lambda h, i: (h, i, 0)), every]
        + [every] * (not first)
        + [anywhere] * len(weights),
        out_specs=[pl.BlockSpec((None, block // 2, wide), lambda h, i: (h, i, 0)), every]
        + [anywhere] * len(weights),
        out_shape=[
            jax.ShapeDtypeStruct((heads, tgt // 2, wide), BF16),
            jax.ShapeDtypeStruct((heads, src, wide), BF16 if last else F32),
        ]
        + [pltpu.VMEM(w.shape, w.dtype) for w in weights],
        scratch_shapes=[pltpu.SemaphoreType.DMA((2,))] * last
        + [
            pltpu.VMEM((src, tile), F32),
            pltpu.VMEM((src, tile), F32),
            pltpu.VMEM((src, tile), F32),
            pltpu.VMEM((src, wide), F32),
            pltpu.VMEM((HD, src), BF16),
        ],
        compiler_params=pltpu.CompilerParams(vmem_limit_bytes=32 * MIB),
        cost_estimate=pl.CostEstimate(
            flops=5 * 8 * work * HD, bytes_accessed=8 * heads * (tgt + src) * wide, transcendentals=work
        ),
    )(qg, kv, *(() if first else (before,)), *weights)


def local(seq, col, memory, query, out_grad, w_key, w_value):
    tgt, width = query.shape
    heads = width // HD
    groups = math.gcd(heads, seq)
    ranges = seq // groups
    each = heads // groups
    same_range = [[r * groups + g for g in range(groups)] for r in range(ranges)]
    same_heads = [[r * groups + g for r in range(ranges)] for g in range(groups)]
    pairwise = ranges == 1 and each == 1 and groups >= 16 and groups & (groups - 1) == 0
    me = lax.axis_index("seq").astype(jnp.int32) if pairwise else jnp.int32(0)
    me = me.reshape(1)
    far = groups // 4

    def deal(x):
        return lax.all_to_all(x, "seq", 0, 0, tiled=True, axis_index_groups=same_range)

    def swap(x, bits):
        return lax.ppermute(x, "seq", [(i, i ^ bits) for i in range(seq)])

    def gather_far(x, d):
        return swap(x, 4 * d) if d else x

    def by_head(x, many):
        x = x.reshape(many, each, *x.shape[1:]).swapaxes(0, 1)
        return x.reshape(each, many * x.shape[2], x.shape[3])

    def by_owner(x, many):
        x = x.reshape(each, many, x.shape[1] // many, x.shape[2]).swapaxes(0, 1)
        return x.reshape(many * each, *x.shape[2:])

    def shift(x, by):
        return lax.ppermute(x, "col", [(i, (i + by) % col) for i in range(col)])

    rows = memory.shape[0] // seq
    total = rows * col
    own = lax.all_to_all(memory.reshape(seq, rows, -1), "seq", 0, 0, tiled=True)

    if pairwise:
        early = far // 2
        late = [d for d in range(far) if d != early]
        kept, left, kept_late, left_late = pair_targets(query, out_grad, me, [[early], late])
        kept, left = cross(kept, swap(left, 2))
        early_qg, own = lax.optimization_barrier((join(kept, [swap(x, 1) for x in left])[0], own))
        early_qg = gather_far(early_qg, early)
        left_late = concat([left_late], after=(own,))
        left_late = swap(left_late, 2)
        held = fetch([w_key, w_value], after=(own,))
        kept, left = cross(kept_late, left_late, after=held[:1])
        late_qg = join(kept, [swap(x, 1) for x in left])
        half = seq // 2
        rest = [[shift(x, by) for by in range(1, col)] for x in (own[:half], own[half:])]
        sums = project_half(own, rest[0], *held, 0)
        kv = project_half(own, rest[1], *held, half, sums, after=(late_qg[0],))[0]
        early_qg, kv = lax.optimization_barrier((early_qg, kv))
        kv = deal(kv)
        late_qg = [gather_far(x, d) for x, d in zip(late_qg, late)]
        qg = [[late_qg[0], early_qg], late_qg[1:]]
    else:
        qg = deal(pair_heads(query, out_grad))
        kv = deal(project([own, *[shift(own, by) for by in range(1, col)]], w_key, w_value))
        qg = [by_head(qg, groups)]
    if ranges > 1:
        kv = lax.all_gather(kv, "seq", axis=0, tiled=True, axis_index_groups=same_heads)
    kv = by_head(kv, seq)

    dq, dkv = [], None
    for i, x in enumerate(qg):
        if pairwise:
            x = concat([piece.reshape(-1, 2 * HD) for piece in x], after=(dkv,) * (i > 0))[None]
        weights = (w_key, w_value) if i == len(qg) - 1 else ()
        part, dkv, *weights = attention(x, kv, tgt, dkv, weights)
        dq.append(part)
        if pairwise and i == 0:
            home, away = dq.pop().reshape(2, 2, 2, tgt // 2, 2 * HD)
            away = gather_far(away, early)
    w_key, w_value = weights
    if pairwise:
        dkv, away = lax.optimization_barrier((dkv, away))
    dkv = by_owner(dkv, seq)
    if ranges > 1:
        dkv = lax.psum_scatter(dkv, "seq", scatter_dimension=0, tiled=True, axis_index_groups=same_heads)
    dkv = deal(dkv)

    others = [
        (by, memory_grad(dkv, by * rows, rows, w_key, w_value, seq, BF16, span))
        for by in range(1, col)
        for span in ((0, 0.5), (0.5, 1))
    ]
    first = [x for _, x in others]
    others = [shift(x, col - by) for by, x in others]
    mine = memory_grad(dkv, 0, rows, w_key, w_value, seq, F32)
    if pairwise:
        dq = concat([x.reshape(-1, 2, 2, tgt // 2, 2 * HD) for x in dq], after=first)
        dq = [home, *[gather_far(x, d) for x, d in zip(dq, late[1:])]]
        dq.insert(early, away)
        summed = add_up(mine, others, after=dq)
        kept, left = part_ways(dq, after=(summed,))
        kept, left = cross(kept, swap(left, 1))
        dq = unpack_query_grad(kept, swap(concat([x[None] for x in left]), 2), me)
    else:
        summed = add_up(mine, others)
        dq = deal(by_owner(dq[0], groups))
        dq = dq.reshape(heads, tgt // 2, 2, HD).transpose(2, 1, 0, 3).reshape(tgt, width)
    d_memory = lax.all_to_all(summed, "seq", 0, 0, tiled=True)
    return dq, d_memory.reshape(memory.shape)


def solution(mesh):
    return jax.shard_map(
        functools.partial(local, mesh.shape["seq"], mesh.shape["col"]),
        mesh=mesh,
        in_specs=(
            P("col", "seq"),
            P("seq", "col"),
            P("seq", "col"),
            P(None, "col"),
            P(None, "col"),
        ),
        out_specs=(P("seq", "col"), P("col", "seq")),
        check_vma=False,
    )
```
